512 devices in a mesh: tile: 64 (over y, z_hi, x), lev: 8 (over z_lo, core).
Axes of the slice: x: 4, y: 8, z: 8 (z_hi: 2, z_lo: 4; z = z_hi * 4 + z_lo), core: 2. Of those that a mesh axis runs over, the one named last changes fastest.
Arguments:
- adjoint: float32 [4, 32, 2048, 256], P(None, 'lev', 'tile'), may hold values from -6 to 6
- wind_x: float32 [32, 2048, 256], P('lev', 'tile'), may hold values from -0.25 to 0.25
- wind_y: float32 [32, 2048, 256], P('lev', 'tile'), may hold values from -0.25 to 0.25
- kz: float32 [32, 2048, 256], P('lev', 'tile'), may hold values from 10 to 400
- forcing: float32 [64, 64, 4, 32, 32], P('tile', None, None, 'lev'), may hold values from -6 to 6
- mon_cols: int32 [64, 64, 32], P('tile'), may hold values from 0 to 8191
- mon_counts: int32 [64, 64], P('tile'), may hold values from 0 to 32, as said below
Outputs:
- updated: float32 [4, 32, 2048, 256], P(None, 'lev', 'tile')
The draws below stay inside these ranges and needn't reach their ends.
Inputs may be any that keep to these rules, and one draw needn't show every extreme that they name: `mon_counts`: in every draw one owning strip has all 32 slots used from every sending strip.
All inputs are finite; a program needn't handle non-finite values.
Results may differ from the reference program's by a relative error of at most 0.00016.
Values sent between devices are 32-bit elements; how exact they have to be, the bound alone decides.
No kernel may reach another device: no remote copies, remote signals or barrier semaphores. Data moves between devices by JAX's collectives and lax.ppermute only.
A program may use at most 128 MiB of HBM per device.

```python
import math
import jax
import jax.numpy as jnp
from jax import lax

TRACERS = 4
LON_DEV = 32
NLAT = 256
CAP = 32
TILES = 64
NLEV = 32
NLON = 2048


def draw_mon_counts(key, part):
    key = jax.random.fold_in(key, 11)
    key_counts, key_busiest = jax.random.split(key)
    base_counts = jax.random.randint(key_counts, (TILES, TILES), 0, CAP + 1)
    busiest = jax.random.randint(key_busiest, (), 0, TILES)
    owner_id = jnp.arange(TILES)[None, :]
    return jnp.where(owner_id == busiest, CAP, base_counts).astype(jnp.int32)


def with_ends(values, key, least, largest):
    longest = values.shape.index(max(values.shape))
    spots = []
    for shift in (0, 1):
        where = [jax.random.randint(jax.random.fold_in(key, axis), (), 0, length) for axis, length in enumerate(values.shape)]
        where[longest] = (where[longest] + shift) % values.shape[longest]
        spots.append(tuple(where))
    return values.at[spots[0]].set(least).at[spots[1]].set(largest)


def steps_of(own_key, dims, pieces, smallest, high):
    loudness, own = 1.0, jax.random.fold_in(own_key, 6)
    for position, shards_of in pieces:
        draws = jnp.exp(jax.random.uniform(jax.random.fold_in(own, position), (shards_of,), jnp.float32, smallest / len(pieces), high / len(pieces)))
        loudness = loudness * jnp.repeat(draws, dims[position] // shards_of).reshape([-1 if axis == position else 1 for axis in range(len(dims))])
    return loudness


def scatter_about(own_key, shape, width, limit, pieces=(), dtype=jnp.bfloat16):
    entries = jax.random.normal(own_key, shape, jnp.float32) * width
    if len(pieces) > 0:
        entries = steps_of(own_key, shape, pieces, -0.22, 0.18) * entries
    return jnp.clip(entries, min=-limit, max=limit).astype(dtype)


def setup_inputs(seed: int = 0) -> dict:
    keys = jax.random.split(jax.random.key(seed), 8)
    return {
        "adjoint": scatter_about(keys[0], (TRACERS, NLEV, NLON, NLAT), 1.0, 6.0, ((1, 8), (2, 64)), jnp.float32),
        "wind_x": jnp.clip(jax.random.uniform(keys[1], (NLEV, NLON, NLAT), jnp.float32, -0.25, 0.25) * steps_of(keys[1], (NLEV, NLON, NLAT), ((0, 8), (1, 64)), -0.4, 0.0), -0.25, 0.25),
        "wind_y": jnp.clip(jax.random.uniform(keys[2], (NLEV, NLON, NLAT), jnp.float32, -0.25, 0.25) * steps_of(keys[2], (NLEV, NLON, NLAT), ((0, 8), (1, 64)), -0.4, 0.0), -0.25, 0.25),
        "kz": jnp.clip(jnp.exp(math.log(400.0) - 3.6888795 * jax.random.uniform(keys[3], (NLEV, NLON, NLAT), jnp.float32) ** steps_of(keys[3], (NLEV, NLON, NLAT), ((0, 8), (1, 64)), -0.2, 0.2)), 10.0, 400.0),
        "forcing": scatter_about(keys[4], (TILES, TILES, TRACERS, NLEV, CAP), 1.0, 6.0, ((0, 64), (3, 8)), jnp.float32),
        "mon_cols": with_ends(jax.random.randint(keys[5], (TILES, TILES, CAP), 0, LON_DEV * NLAT), jax.random.fold_in(keys[5], 1), 0, (LON_DEV * NLAT) - 1).astype(jnp.int32),
        "mon_counts": draw_mon_counts(jax.random.fold_in(keys[7], 71), 0),
    }


def tri_solve(lower_band, main_band, upper_band, right_side):
    count_levels = right_side.shape[1]
    ratios = []
    scaled = []
    for level_id in range(count_levels):
        if level_id == 0:
            pivot_value = main_band[0]
            scaled.append(right_side[:, 0] / pivot_value)
        else:
            pivot_value = main_band[level_id] - lower_band[level_id] * ratios[level_id - 1]
            scaled.append((right_side[:, level_id] - lower_band[level_id] * scaled[level_id - 1]) / pivot_value)
        ratios.append(upper_band[level_id] / pivot_value)
    solution = [scaled[-1]]
    for level_id in range(count_levels - 2, -1, -1):
        solution.append(scaled[level_id] - ratios[level_id] * solution[-1])
    return jnp.stack(solution[::-1], 1)


def column_system(coupling, coupling_first):
    coupling_below = jnp.concatenate([coupling_first[None], coupling[:-1]], 0)
    return -coupling_below, 1.0 + coupling_below + coupling, -coupling


def transport(field, wind_east, wind_west, wind_y, east_side, west_side):
    lat_count = field.shape[-1]
    latitude = lax.broadcasted_iota(jnp.int32, wind_y.shape, wind_y.ndim - 1)
    wind_north = jnp.where(latitude == lat_count - 1, 0.0, wind_y)
    wind_south = jnp.pad(wind_north, [(0, 0)] * (wind_y.ndim - 1) + [(1, 0)])[..., :-1]
    north_side = jnp.pad(field, [(0, 0)] * (field.ndim - 1) + [(0, 1)])[..., 1:]
    south_side = jnp.pad(field, [(0, 0)] * (field.ndim - 1) + [(1, 0)])[..., :-1]
    return (field + jnp.maximum(wind_east, 0.0) * (east_side - field)
            - jnp.minimum(wind_west, 0.0) * (west_side - field)
            + jnp.maximum(wind_north, 0.0) * (north_side - field)
            - jnp.minimum(wind_south, 0.0) * (south_side - field))


def reference(adjoint, wind_x, wind_y, kz, forcing, mon_cols, mon_counts):
    east_side = jnp.roll(adjoint, -1, axis=2)
    west_side = jnp.roll(adjoint, 1, axis=2)
    wind_west = jnp.roll(wind_x, 1, axis=1)
    advected = transport(adjoint, wind_x, wind_west, wind_y, east_side, west_side)
    slot_id = lax.broadcasted_iota(jnp.int32, mon_cols.shape, 2)
    owner_id = lax.broadcasted_iota(jnp.int32, mon_cols.shape, 1)
    is_valid = slot_id < mon_counts[:, :, None]
    flat_index = jnp.where(is_valid, owner_id * (LON_DEV * NLAT) + mon_cols, 0).reshape(-1)
    masked_rows = jnp.where(is_valid[:, :, None, None, :], forcing, 0.0)
    masked_rows = jnp.transpose(masked_rows, (2, 3, 0, 1, 4)).reshape(TRACERS, NLEV, -1)
    forced = advected.reshape(TRACERS, NLEV, -1).at[:, :, flat_index].add(masked_rows).reshape(advected.shape)
    level_id = lax.broadcasted_iota(jnp.int32, kz.shape, 0)
    coupling = jnp.where(level_id == NLEV - 1, 0.0, kz)
    lower_band, main_band, upper_band = column_system(coupling, jnp.zeros_like(coupling[0]))
    return tri_solve(lower_band, main_band, upper_band, forced)
```

```python
import jax
import jax.numpy as jnp
from jax import lax
from jax.experimental import pallas as pl
from jax.experimental.pallas import tpu as pltpu
from jax.sharding import PartitionSpec as P

TRACERS = 4
LEV_DEV = 4
NLEV = 32
LON = 32
LAT = 256
TILES = 64
CAP = 32
HALF = LON // 2
ROWS = TRACERS * LEV_DEV
VMEM = pl.BlockSpec(memory_space=pltpu.VMEM)
SMEM = pl.BlockSpec(memory_space=pltpu.SMEM)
F32 = jnp.float32


def call(body, outs, in_specs, scratch=(), limit=12 << 20, flops=0, moved=1 << 20, **more):
    shapes = tuple(jax.ShapeDtypeStruct(shape, F32) for shape in outs)
    return pl.pallas_call(
        body,
        out_shape=shapes,
        in_specs=in_specs,
        out_specs=tuple(VMEM for _ in outs),
        scratch_shapes=list(scratch),
        compiler_params=pltpu.CompilerParams(vmem_limit_bytes=limit),
        cost_estimate=pl.CostEstimate(flops=flops, bytes_accessed=moved, transcendentals=0),
        **more,
    )


def pack_body(force, cols, counts, low_adj, high_adj, high_wind, payload, low, high):
    slot = lax.broadcasted_iota(jnp.int32, (CAP, TILES), 0)
    valid = slot < counts[...]
    lon = jnp.where(valid, cols[...] >> 8, -1).astype(F32)
    lat = (cols[...] & 255).astype(F32)
    rest = jnp.zeros((56, TILES), F32)
    for i in range(8):
        parts = [force[pl.ds(4 * i + g, ROWS, stride=CAP), :] for g in range(4)]
        block = jnp.concatenate(parts + [lon[4 * i : 4 * i + 4], lat[4 * i : 4 * i + 4], rest], 0)
        payload[:, i, :] = block.T
    low[...] = low_adj[:, 0, :]
    high[0:ROWS, :] = high_adj[:, 7, :]
    high[ROWS : ROWS + LEV_DEV, :] = high_wind[:, 7, :]


def pack(forcing, mon_cols, mon_counts, adjoint, wind_x):
    force = jnp.transpose(forcing[0], (1, 2, 3, 0)).reshape(ROWS * CAP, TILES)
    cols = jnp.transpose(mon_cols[0], (1, 0))
    specs = [
        VMEM,
        VMEM,
        VMEM,
        pl.BlockSpec((ROWS, 8, LAT), lambda i: (0, 0, 0)),
        pl.BlockSpec((ROWS, 8, LAT), lambda i: (0, 3, 0)),
        pl.BlockSpec((LEV_DEV, 8, LAT), lambda i: (0, 3, 0)),
    ]
    outs = ((TILES, 8, 128), (ROWS, LAT), (ROWS + LEV_DEV, LAT))
    return call(pack_body, outs, specs, grid=(1,))(force, cols, mon_counts, adjoint, adjoint, wind_x)


def advect_body(adj, wind_x, wind_y, west, east, out):
    row = lax.broadcasted_iota(jnp.int32, (LON, LAT), 0)
    lane = lax.broadcasted_iota(jnp.int32, (LON, LAT), 1)
    for lev in range(LEV_DEV):
        cx = wind_x[lev]
        cx_west = jnp.where(row == 0, west[ROWS + lev : ROWS + lev + 1, :], pltpu.roll(cx, 1, 0))
        cy_n = jnp.where(lane == LAT - 1, 0.0, wind_y[lev])
        cy_s = pltpu.roll(cy_n, 1, 1)
        to_east = jnp.maximum(cx, 0.0)
        to_west = jnp.minimum(cx_west, 0.0)
        to_north = jnp.maximum(cy_n, 0.0)
        to_south = jnp.minimum(cy_s, 0.0)
        for tracer in range(TRACERS):
            n = tracer * LEV_DEV + lev
            a = adj[n]
            a_east = jnp.where(row == LON - 1, east[n : n + 1, :], pltpu.roll(a, LON - 1, 0))
            a_west = jnp.where(row == 0, west[n : n + 1, :], pltpu.roll(a, 1, 0))
            a_north = pltpu.roll(a, LAT - 1, 1)
            a_south = pltpu.roll(a, 1, 1)
            out[n] = (
                a
                + to_east * (a_east - a)
                - to_west * (a_west - a)
                + to_north * (a_north - a)
                - to_south * (a_south - a)
            )


def weights_body(place, kz, up, down, inverse, chip_up, chip_down, core_up, core_down, up_all, down_all, low, high):
    lev = place[0]
    core = lev % 2
    below = jnp.zeros((LON, LAT), F32)
    for l in range(NLEV):
        low[l] = below
        if l < NLEV - 1:
            k = kz[l]
            ground = 1.0 + below
            up_all[l] = k / (ground + k)
            below = up_all[l] * ground
        else:
            up_all[l] = jnp.zeros((LON, LAT), F32)
    above = jnp.zeros((LON, LAT), F32)
    for l in range(NLEV - 1, -1, -1):
        high[l] = above
        if l > 0:
            k = kz[l - 1]
            ground = 1.0 + above
            down_all[l] = k / (ground + k)
            above = down_all[l] * ground
        else:
            down_all[l] = jnp.zeros((LON, LAT), F32)
    mine = pl.ds(lev * LEV_DEV, LEV_DEV)
    up[...] = up_all[mine]
    down[...] = down_all[mine]
    inverse[...] = 1.0 / (1.0 + low[mine] + high[mine])
    half = pl.ds(pl.multiple_of(core * HALF, HALF), HALF)
    for chip in range(4):
        ups = [up_all[8 * chip + n, half, :] for n in range(8)]
        downs = [down_all[8 * chip + n, half, :] for n in range(8)]
        up_low, up_high = (ups[0] * ups[1]) * (ups[2] * ups[3]), (ups[4] * ups[5]) * (ups[6] * ups[7])
        down_low, down_high = (downs[0] * downs[1]) * (downs[2] * downs[3]), (downs[4] * downs[5]) * (downs[6] * downs[7])
        chip_up[chip] = up_low * up_high
        chip_down[chip] = down_low * down_high

        @pl.when(lev // 2 == chip)
        def _():
            core_up[0] = up_low
            core_up[1] = up_high
            core_down[0] = down_low
            core_down[1] = down_high


def force_body(place, received, advected, up, down, forced, own, other, sums):
    core = place[0] % 2
    messages = received[...].reshape(TILES * 8, 128)
    turned = messages.T
    lon_id = lax.broadcasted_iota(jnp.int32, (LON, TILES * 8), 0).astype(F32)
    lat_id = lax.broadcasted_iota(jnp.int32, (TILES * 8, LAT), 1).astype(F32)
    total = jnp.zeros((ROWS * LON, LAT), F32)
    for g in range(4):
        here = lon_id == turned[64 + g : 65 + g, :]
        hot = jnp.where(lat_id == messages[:, 68 + g : 69 + g], 1.0, 0.0).astype(jnp.bfloat16)
        rows = turned[ROWS * g : ROWS * g + ROWS, :]
        coarse = rows.astype(jnp.bfloat16).astype(F32)
        fine = rows - coarse
        for piece in (coarse, fine):
            spread = [jnp.where(here, piece[r : r + 1, :], 0.0).astype(jnp.bfloat16) for r in range(ROWS)]
            total += jnp.dot(jnp.concatenate(spread, 0), hot, preferred_element_type=F32)
    for n in range(ROWS):
        forced[n] = advected[n] + total[n * LON : (n + 1) * LON]
    for tracer in range(TRACERS):
        rising = jnp.zeros((LON, LAT), F32)
        sinking = jnp.zeros((LON, LAT), F32)
        for lev in range(LEV_DEV):
            rising = up[lev] * (forced[tracer * LEV_DEV + lev] + rising)
        for lev in range(LEV_DEV - 1, -1, -1):
            sinking = down[lev] * (forced[tracer * LEV_DEV + lev] + sinking)
        sums[0, tracer] = rising
        sums[1, tracer] = sinking
    mine = pl.ds(pl.multiple_of(core * HALF, HALF), HALF)
    yours = pl.ds(pl.multiple_of((1 - core) * HALF, HALF), HALF)
    for way in range(2):
        for tracer in range(TRACERS):
            own[way, tracer] = sums[way, tracer, mine, :]
            other[way, tracer] = sums[way, tracer, yours, :]


def chip_body(place, own, got, core_up, core_down, blocks):
    chip = place[0] // 2
    first = place[0] % 2 == 0
    for tracer in range(TRACERS):
        rise = [jnp.where(first, own[0, tracer], got[0, tracer]), jnp.where(first, got[0, tracer], own[0, tracer])]
        sink = [jnp.where(first, own[1, tracer], got[1, tracer]), jnp.where(first, got[1, tracer], own[1, tracer])]
        rising = rise[1] + core_up[1] * rise[0]
        sinking = sink[0] + core_down[0] * sink[1]
        for to in range(4):
            blocks[to, tracer] = jnp.where(to > chip, rising, sinking)


def meet_body(place, blocks, own, got, core_up, core_down, chip_up, chip_down, keep, send):
    chip = place[0] // 2
    first = place[0] % 2 == 0
    for tracer in range(TRACERS):
        rising = jnp.zeros((HALF, LAT), F32)
        sinking = jnp.zeros((HALF, LAT), F32)
        for z in range(4):
            rising = jnp.where(z < chip, chip_up[z] * rising + blocks[z, tracer], rising)
        for z in range(3, -1, -1):
            sinking = jnp.where(z > chip, chip_down[z] * sinking + blocks[z, tracer], sinking)
        rise = jnp.where(first, own[0, tracer], got[0, tracer])
        sink = jnp.where(first, got[1, tracer], own[1, tracer])
        rising_mid = rise + core_up[0] * rising
        sinking_mid = sink + core_down[1] * sinking
        keep[0, tracer] = jnp.where(first, rising, rising_mid)
        keep[1, tracer] = jnp.where(first, sinking_mid, sinking)
        send[0, tracer] = jnp.where(first, rising_mid, rising)
        send[1, tracer] = jnp.where(first, sinking, sinking_mid)


def solve_body(place, forced, keep, got, up, down, inverse, out):
    first = place[0] % 2 == 0

    def whole(way, tracer):
        mine, yours = keep[way, tracer], got[way, tracer]
        return jnp.concatenate([jnp.where(first, mine, yours), jnp.where(first, yours, mine)], 0)

    for tracer in range(TRACERS):
        rising, sinking = whole(0, tracer), whole(1, tracer)
        partial = []
        for lev in range(LEV_DEV):
            partial.append(forced[tracer * LEV_DEV + lev] + rising)
            rising = up[lev] * partial[lev]
        for lev in range(LEV_DEV - 1, -1, -1):
            out[tracer * LEV_DEV + lev] = (partial[lev] + sinking) * inverse[lev]
            sinking = down[lev] * (forced[tracer * LEV_DEV + lev] + sinking)


def per_device(adjoint, wind_x, wind_y, kz, forcing, mon_cols, mon_counts):
    place = lax.axis_index("lev").astype(jnp.int32).reshape(1)
    field = adjoint.reshape(ROWS, LON, LAT)
    tiles = [(i, (i + 1) % TILES) for i in range(TILES)]
    cores = [(i, i ^ 1) for i in range(8)]
    chips = [[0, 2, 4, 6], [1, 3, 5, 7]]

    kz_all = lax.all_gather(kz, "lev", axis=0, tiled=True)
    payload, low, high = pack(forcing, mon_cols, mon_counts, field, wind_x)
    received = lax.all_to_all(payload, "tile", 0, 0, tiled=True)
    west = lax.ppermute(high, "tile", tiles)
    east = lax.ppermute(low, "tile", [(j, i) for i, j in tiles])

    (advected,) = call(advect_body, ((ROWS, LON, LAT),), [VMEM] * 5, moved=2 << 20)(field, wind_x, wind_y, west, east)
    level = (LEV_DEV, LON, LAT)
    pair = (2, TRACERS, HALF, LAT)
    every = pltpu.VMEM((NLEV, LON, LAT), F32)
    up, down, inverse, chip_up, chip_down, core_up, core_down = call(
        weights_body,
        (level, level, level, (4, HALF, LAT), (4, HALF, LAT), (2, HALF, LAT), (2, HALF, LAT)),
        [SMEM, VMEM],
        [every] * 4,
        moved=3 << 20,
    )(place, kz_all)
    forced, own, other = call(
        force_body,
        ((ROWS, LON, LAT), pair, pair),
        [SMEM] + [VMEM] * 4,
        [pltpu.VMEM((2, TRACERS, LON, LAT), F32)],
        limit=24 << 20,
        moved=2 << 20,
    )(place, received, advected, up, down)
    got = lax.ppermute(other, "lev", cores)
    (blocks,) = call(chip_body, ((4, TRACERS, HALF, LAT),), [SMEM] + [VMEM] * 4)(place, own, got, core_up, core_down)
    arrived = lax.all_to_all(blocks, "lev", 0, 0, tiled=True, axis_index_groups=chips)
    keep, send = call(meet_body, (pair, pair), [SMEM] + [VMEM] * 7)(
        place, arrived, own, got, core_up, core_down, chip_up, chip_down
    )
    back = lax.ppermute(send, "lev", cores)
    (updated,) = call(solve_body, ((ROWS, LON, LAT),), [SMEM] + [VMEM] * 6)(
        place, forced, keep, back, up, down, inverse
    )
    return updated.reshape(adjoint.shape)


def solution(mesh):
    in_specs = (
        P(None, "lev", "tile", None),
        P("lev", "tile", None),
        P("lev", "tile", None),
        P("lev", "tile", None),
        P("tile", None, None, "lev", None),
        P("tile", None, None),
        P("tile", None),
    )
    out_specs = P(None, "lev", "tile", None)
    return jax.shard_map(
        per_device, mesh=mesh, in_specs=in_specs, out_specs=out_specs, check_vma=False
    )
```

```python
import jax
import jax.numpy as jnp
from jax import lax
from jax.experimental import pallas as pl
from jax.experimental.pallas import tpu as pltpu
from jax.sharding import PartitionSpec as P

TRACERS = 4
LEV_DEV = 4
LEVS = 8
NLEV = 32
LON = 32
LAT = 256
TILES = 64
CAP = 32
HALF = LON // 2
ROWS = TRACERS * LEV_DEV
VMEM = pl.BlockSpec(memory_space=pltpu.VMEM)
HBM = pl.BlockSpec(memory_space=pltpu.HBM)
SMEM = pl.BlockSpec(memory_space=pltpu.SMEM)
F32 = jnp.float32


def call(body, outs, in_specs, scratch=(), limit=12 << 20, flops=0, moved=1 << 20, **more):
    shapes = tuple(jax.ShapeDtypeStruct(shape, F32) for shape in outs)
    return pl.pallas_call(
        body,
        out_shape=shapes,
        in_specs=in_specs,
        out_specs=tuple(VMEM for _ in outs),
        scratch_shapes=list(scratch),
        compiler_params=pltpu.CompilerParams(vmem_limit_bytes=limit),
        cost_estimate=pl.CostEstimate(flops=flops, bytes_accessed=moved, transcendentals=0),
        **more,
    )


def pack_body(place, force, cols, counts, adj, wind, payload, first, second, force_v, cols_v, counts_v, low_v, high_v, wind_v, sems):
    last = pl.ds(LON - 8, 8)
    copies = [
        pltpu.make_async_copy(force, force_v, sems.at[0]),
        pltpu.make_async_copy(cols, cols_v, sems.at[1]),
        pltpu.make_async_copy(counts, counts_v, sems.at[2]),
        pltpu.make_async_copy(adj.at[:, pl.ds(0, 8), :], low_v, sems.at[3]),
        pltpu.make_async_copy(adj.at[:, last, :], high_v, sems.at[4]),
        pltpu.make_async_copy(wind.at[:, last, :], wind_v, sems.at[5]),
    ]
    for copy in copies:
        copy.start()
    for copy in copies:
        copy.wait()
    for k in range(4):
        parts = [force_v[pl.ds(8 * k + g, ROWS, stride=CAP), :] for g in range(8)]
        payload[:, 0, 128 * k : 128 * (k + 1)] = jnp.concatenate(parts, 0).T
    slot = lax.broadcasted_iota(jnp.int32, (CAP, TILES), 0)
    lon = jnp.where(slot < counts_v[...], cols_v[...] >> 8, -1).astype(F32)
    lat = (cols_v[...] & 255).astype(F32)
    payload[:, 0, 512:640] = jnp.concatenate([lon, lat, jnp.zeros((64, TILES), F32)], 0).T
    even = place[0] % 2 == 0
    low, high, cx = low_v[:, 0, :], high_v[:, 7, :], wind_v[:, 7, :]
    first[0:ROWS, :] = jnp.where(even, high, low)
    second[0:ROWS, :] = jnp.where(even, low, high)
    first[ROWS : ROWS + LEV_DEV, :] = cx
    second[ROWS : ROWS + LEV_DEV, :] = cx


def pack(tile, forcing, mon_cols, mon_counts, field, wind_x):
    force = jnp.transpose(forcing[0], (1, 2, 3, 0)).reshape(ROWS * CAP, TILES)
    cols = jnp.transpose(mon_cols[0], (1, 0))
    edge = (ROWS + LEV_DEV, LAT)
    scratch = [
        pltpu.VMEM((ROWS * CAP, TILES), F32),
        pltpu.VMEM((CAP, TILES), jnp.int32),
        pltpu.VMEM((1, TILES), jnp.int32),
        pltpu.VMEM((ROWS, 8, LAT), F32),
        pltpu.VMEM((ROWS, 8, LAT), F32),
        pltpu.VMEM((LEV_DEV, 8, LAT), F32),
        pltpu.SemaphoreType.DMA((6,)),
    ]
    operands = [pltpu.with_memory_space_constraint(x, pltpu.HBM) for x in (force, cols, mon_counts, field, wind_x)]
    return call(pack_body, ((TILES, 1, 640), edge, edge), [SMEM] + [HBM] * 5, scratch)(tile, *operands)


def advect_body(place, adj, wind_x, wind_y, first, second, out):
    even = place[0] % 2 == 0
    west = jnp.where(even, second[...], first[...])
    east = jnp.where(even, first[...], second[...])
    row = lax.broadcasted_iota(jnp.int32, (LON, LAT), 0)
    lane = lax.broadcasted_iota(jnp.int32, (LON, LAT), 1)
    for lev in range(LEV_DEV):
        cx = wind_x[lev]
        cx_west = jnp.where(row == 0, west[ROWS + lev : ROWS + lev + 1, :], pltpu.roll(cx, 1, 0))
        cy_n = jnp.where(lane == LAT - 1, 0.0, wind_y[lev])
        cy_s = pltpu.roll(cy_n, 1, 1)
        to_east = jnp.maximum(cx, 0.0)
        to_west = jnp.minimum(cx_west, 0.0)
        to_north = jnp.maximum(cy_n, 0.0)
        to_south = jnp.minimum(cy_s, 0.0)
        for tracer in range(TRACERS):
            n = tracer * LEV_DEV + lev
            a = adj[n]
            a_east = jnp.where(row == LON - 1, east[n : n + 1, :], pltpu.roll(a, LON - 1, 0))
            a_west = jnp.where(row == 0, west[n : n + 1, :], pltpu.roll(a, 1, 0))
            a_north = pltpu.roll(a, LAT - 1, 1)
            a_south = pltpu.roll(a, 1, 1)
            out[n] = (
                a
                + to_east * (a_east - a)
                - to_west * (a_west - a)
                + to_north * (a_north - a)
                - to_south * (a_south - a)
            )


def block_body(place, kz, carry, ports):
    shunt = jnp.ones((LON, LAT), F32)
    series = kz[0]
    top = jnp.zeros((LON, LAT), F32)
    for lev in range(1, LEV_DEV):
        k = kz[lev]
        if lev == LEV_DEV - 1:
            k = jnp.where(place[0] == LEVS - 1, 0.0, k)
        ground = 1.0 + top
        inverse = 1.0 / (series + k + ground)
        below, above = series * inverse, k * inverse
        carry[0, lev - 1] = below
        carry[1, lev - 1] = above
        carry[2, lev - 1] = inverse
        shunt = shunt + below * ground
        top = above * ground
        series = below * k
    ports[0] = shunt
    ports[1] = series
    ports[2] = top


def chunks(array):
    return [array[8 * (w // 2) : 8 * (w // 2) + 8, 128 * (w % 2) : 128 * (w % 2) + 128] for w in range(LEVS)]


def force_body(received, advected, carry, ports, inner, blocks):
    data = jnp.concatenate([received[:, 0, 128 * k : 128 * (k + 1)] for k in range(4)], 0)
    where = received[:, 0, 512:640]
    where = jnp.concatenate([where] + [pltpu.roll(where, 128 - 8 * k, 1) for k in range(1, 4)], 0)
    rows_all, lons = data.T, where.T
    lon_id = lax.broadcasted_iota(jnp.int32, (LON, 4 * TILES), 0).astype(F32)
    lat_id = lax.broadcasted_iota(jnp.int32, (4 * TILES, LAT), 1).astype(F32)
    total = jnp.zeros((ROWS * LON, LAT), F32)
    for g in range(8):
        here = lon_id == lons[g : g + 1, :]
        hot = jnp.where(lat_id == where[:, CAP + g : CAP + g + 1], 1.0, 0.0).astype(jnp.bfloat16)
        rows = rows_all[ROWS * g : ROWS * g + ROWS, :]
        coarse = rows.astype(jnp.bfloat16).astype(F32)
        fine = rows - coarse
        for piece in (coarse, fine):
            spread = [jnp.where(here, piece[r : r + 1, :], 0.0).astype(jnp.bfloat16) for r in range(ROWS)]
            total += jnp.dot(jnp.concatenate(spread, 0), hot, preferred_element_type=F32)
    for tracer in range(TRACERS):
        forced = []
        for lev in range(LEV_DEV):
            n = tracer * LEV_DEV + lev
            forced.append(advected[n] + total[n * LON : (n + 1) * LON])
        low = forced[0]
        high = jnp.zeros((LON, LAT), F32)
        for lev in range(1, LEV_DEV):
            middle = high + forced[lev]
            low = low + carry[0, lev - 1] * middle
            high = carry[1, lev - 1] * middle
            inner[tracer, lev - 1] = carry[2, lev - 1] * middle
        for w, (piece_low, piece_high) in enumerate(zip(chunks(low), chunks(high))):
            blocks[w, tracer] = piece_low
            blocks[w, TRACERS + tracer] = piece_high
    for n in range(3):
        for w, piece in enumerate(chunks(ports[n])):
            blocks[w, 2 * TRACERS + n] = piece


def chain_body(blocks, ends):
    zero = jnp.zeros((8, 128), F32)
    below, rising = [zero], [[zero] * TRACERS]
    for p in range(LEVS - 1):
        shunt, series, top = [blocks[p, 2 * TRACERS + n] for n in range(3)]
        ground = shunt + below[p]
        share = series / (series + ground)
        below.append(top + share * ground)
        rising.append([blocks[p, TRACERS + t] + share * (blocks[p, t] + rising[p][t]) for t in range(TRACERS)])
    above, sinking = zero, [zero] * TRACERS
    for p in range(LEVS - 1, -1, -1):
        shunt, series, top = [blocks[p, 2 * TRACERS + n] for n in range(3)]
        if p == LEVS - 1:
            above, sinking = shunt, [blocks[p, t] for t in range(TRACERS)]
        else:
            ground = top + above
            share = series / (series + ground)
            above = shunt + share * ground
            sinking = [blocks[p, t] + share * (blocks[p, TRACERS + t] + sinking[t]) for t in range(TRACERS)]
        inverse = 1.0 / (below[p] + above)
        for t in range(TRACERS):
            value = (rising[p][t] + sinking[t]) * inverse
            ends[p, t] = value
            if p > 0:
                ends[p - 1, TRACERS + t] = value
            if p == LEVS - 1:
                ends[p, TRACERS + t] = zero


def solve_body(inner, ends, carry, out):
    def whole(n):
        return jnp.concatenate([jnp.concatenate([ends[2 * a, n], ends[2 * a + 1, n]], 1) for a in range(4)], 0)

    for tracer in range(TRACERS):
        bottom, level = whole(tracer), whole(TRACERS + tracer)
        for lev in range(LEV_DEV - 1, 0, -1):
            level = inner[tracer, lev - 1] + carry[0, lev - 1] * bottom + carry[1, lev - 1] * level
            out[tracer * LEV_DEV + lev] = level
        out[tracer * LEV_DEV] = bottom


def per_device(adjoint, wind_x, wind_y, kz, forcing, mon_cols, mon_counts):
    place = lax.axis_index("lev").astype(jnp.int32).reshape(1)
    tile = lax.axis_index("tile").astype(jnp.int32).reshape(1)
    field = adjoint.reshape(ROWS, LON, LAT)
    inside = (LEV_DEV - 1, LON, LAT)

    payload, first, second = pack(tile, forcing, mon_cols, mon_counts, field, wind_x)
    received = lax.all_to_all(payload, "tile", 0, 0, tiled=True)
    first = lax.ppermute(first, "tile", [(i, i ^ 1) for i in range(TILES)])
    second = lax.ppermute(second, "tile", [(i, (i + 1 if i % 2 else i - 1) % TILES) for i in range(TILES)])
    carry, ports = call(block_body, ((3,) + inside, (3, LON, LAT)), [SMEM, VMEM])(place, kz)
    (advected,) = call(advect_body, ((ROWS, LON, LAT),), [SMEM] + [VMEM] * 5, moved=2 << 20)(
        tile, field, wind_x, wind_y, first, second
    )
    inner, blocks = call(
        force_body,
        ((TRACERS,) + inside, (LEVS, 11, 8, 128)),
        [VMEM] * 4,
        limit=24 << 20,
        moved=2 << 20,
    )(received, advected, carry, ports)
    arrived = lax.all_to_all(blocks, "lev", 0, 0, tiled=True)
    (ends,) = call(chain_body, ((LEVS, 2 * TRACERS, 8, 128),), [VMEM])(arrived)
    ends = lax.all_to_all(ends, "lev", 0, 0, tiled=True)
    (updated,) = call(solve_body, ((ROWS, LON, LAT),), [VMEM] * 3)(inner, ends, carry)
    return updated.reshape(adjoint.shape)


def solution(mesh):
    in_specs = (
        P(None, "lev", "tile", None),
        P("lev", "tile", None),
        P("lev", "tile", None),
        P("lev", "tile", None),
        P("tile", None, None, "lev", None),
        P("tile", None, None),
        P("tile", None),
    )
    out_specs = P(None, "lev", "tile", None)
    return jax.shard_map(
        per_device, mesh=mesh, in_specs=in_specs, out_specs=out_specs, check_vma=False
    )
```

```python
import jax
import jax.numpy as jnp
from jax import lax
from jax.experimental import pallas as pl
from jax.experimental.pallas import tpu as pltpu
from jax.sharding import PartitionSpec as P

TRACERS = 4
LEV_DEV = 4
LEVS = 8
NLEV = 32
LON = 32
LAT = 256
TILES = 64
CAP = 32
HALF = LON // 2
ROWS = TRACERS * LEV_DEV
VMEM = pl.BlockSpec(memory_space=pltpu.VMEM)
HBM = pl.BlockSpec(memory_space=pltpu.HBM)
SMEM = pl.BlockSpec(memory_space=pltpu.SMEM)
F32 = jnp.float32


def call(body, outs, in_specs, scratch=(), limit=12 << 20, flops=0, moved=1 << 20, out_spec=VMEM, **more):
    shapes = tuple(jax.ShapeDtypeStruct(shape, F32) for shape in outs)
    return pl.pallas_call(
        body,
        out_shape=shapes,
        in_specs=in_specs,
        out_specs=tuple(out_spec for _ in outs),
        scratch_shapes=list(scratch),
        compiler_params=pltpu.CompilerParams(vmem_limit_bytes=limit),
        cost_estimate=pl.CostEstimate(flops=flops, bytes_accessed=moved, transcendentals=0),
        **more,
    )


def pack_body(place, force, cols, counts, adj, wind, payload, first, second, force_v, cols_v, counts_v, low_v, high_v, wind_v, sems):
    last = pl.ds(LON - 8, 8)
    copies = [
        pltpu.make_async_copy(force, force_v, sems.at[0]),
        pltpu.make_async_copy(cols, cols_v, sems.at[1]),
        pltpu.make_async_copy(counts, counts_v, sems.at[2]),
        pltpu.make_async_copy(adj.at[:, pl.ds(0, 8), :], low_v, sems.at[3]),
        pltpu.make_async_copy(adj.at[:, last, :], high_v, sems.at[4]),
        pltpu.make_async_copy(wind.at[:, last, :], wind_v, sems.at[5]),
    ]
    for copy in copies:
        copy.start()
    for copy in copies:
        copy.wait()
    for k in range(4):
        parts = [force_v[pl.ds(8 * k + g, ROWS, stride=CAP), :] for g in range(8)]
        payload[pl.ds(k, TILES, stride=5), :] = jnp.concatenate(parts, 0).T
    slot = lax.broadcasted_iota(jnp.int32, (CAP, TILES), 0)
    lon = jnp.where(slot < counts_v[...], cols_v[...] >> 8, -1).astype(F32)
    lat = (cols_v[...] & 255).astype(F32)
    payload[pl.ds(4, TILES, stride=5), :] = jnp.concatenate([lon, lat, jnp.zeros((64, TILES), F32)], 0).T
    even = place[0] % 2 == 0
    low, high, cx = low_v[:, 0, :], high_v[:, 7, :], wind_v[:, 7, :]
    first[0:ROWS, :] = jnp.where(even, high, low)
    second[0:ROWS, :] = jnp.where(even, low, high)
    first[ROWS : ROWS + LEV_DEV, :] = cx
    second[ROWS : ROWS + LEV_DEV, :] = cx


def pack(tile, forcing, mon_cols, mon_counts, field, wind_x):
    force = jnp.transpose(forcing[0], (1, 2, 3, 0)).reshape(ROWS * CAP, TILES)
    cols = jnp.transpose(mon_cols[0], (1, 0))
    edge = (ROWS + LEV_DEV, LAT)
    scratch = [
        pltpu.VMEM((ROWS * CAP, TILES), F32),
        pltpu.VMEM((CAP, TILES), jnp.int32),
        pltpu.VMEM((1, TILES), jnp.int32),
        pltpu.VMEM((ROWS, 8, LAT), F32),
        pltpu.VMEM((ROWS, 8, LAT), F32),
        pltpu.VMEM((LEV_DEV, 8, LAT), F32),
        pltpu.SemaphoreType.DMA((6,)),
    ]
    operands = [pltpu.with_memory_space_constraint(x, pltpu.HBM) for x in (force, cols, mon_counts, field, wind_x)]
    return call(pack_body, ((TILES * 5, 128), edge, edge), [SMEM] + [HBM] * 5, scratch)(tile, *operands)


def advect_body(adj, wind_x, wind_y, out):
    row = lax.broadcasted_iota(jnp.int32, (LON, LAT), 0)
    lane = lax.broadcasted_iota(jnp.int32, (LON, LAT), 1)
    for lev in range(LEV_DEV):
        cx = wind_x[lev]
        cy_n = jnp.where(lane == LAT - 1, 0.0, wind_y[lev])
        cy_s = pltpu.roll(cy_n, 1, 1)
        to_east = jnp.where(row == LON - 1, 0.0, jnp.maximum(cx, 0.0))
        to_west = jnp.where(row == 0, 0.0, jnp.minimum(pltpu.roll(cx, 1, 0), 0.0))
        to_north = jnp.maximum(cy_n, 0.0)
        to_south = jnp.minimum(cy_s, 0.0)
        for tracer in range(TRACERS):
            n = tracer * LEV_DEV + lev
            a = adj[n]
            out[n] = (
                a
                + to_east * (pltpu.roll(a, LON - 1, 0) - a)
                - to_west * (pltpu.roll(a, 1, 0) - a)
                + to_north * (pltpu.roll(a, LAT - 1, 1) - a)
                - to_south * (pltpu.roll(a, 1, 1) - a)
            )


def block_body(place, kz, carry, ports):
    shunt = jnp.ones((LON, LAT), F32)
    series = kz[0]
    top = jnp.zeros((LON, LAT), F32)
    for lev in range(1, LEV_DEV):
        k = kz[lev]
        if lev == LEV_DEV - 1:
            k = jnp.where(place[0] == LEVS - 1, 0.0, k)
        ground = 1.0 + top
        inverse = 1.0 / (series + k + ground)
        below, above = series * inverse, k * inverse
        carry[0, lev - 1] = below
        carry[1, lev - 1] = above
        carry[2, lev - 1] = inverse
        shunt = shunt + below * ground
        top = above * ground
        series = below * k
    ports[0] = shunt
    ports[1] = series
    ports[2] = top


def chunks(array):
    return [array[8 * (w // 2) : 8 * (w // 2) + 8, 128 * (w % 2) : 128 * (w % 2) + 128] for w in range(LEVS)]


def force_body(received, advected, forced):
    data = jnp.concatenate([received[pl.ds(k, TILES, stride=5), :] for k in range(4)], 0)
    where = received[pl.ds(4, TILES, stride=5), :]
    where = jnp.concatenate([where] + [pltpu.roll(where, 128 - 8 * k, 1) for k in range(1, 4)], 0)
    rows_all, lons = data.T, where.T
    lon_id = lax.broadcasted_iota(jnp.int32, (LON, 4 * TILES), 0).astype(F32)
    lat_id = lax.broadcasted_iota(jnp.int32, (4 * TILES, LAT), 1).astype(F32)
    total = jnp.zeros((ROWS * LON, LAT), F32)
    for g in range(8):
        here = lon_id == lons[g : g + 1, :]
        hot = jnp.where(lat_id == where[:, CAP + g : CAP + g + 1], 1.0, 0.0).astype(jnp.bfloat16)
        rows = rows_all[ROWS * g : ROWS * g + ROWS, :]
        coarse = rows.astype(jnp.bfloat16).astype(F32)
        fine = rows - coarse
        for piece in (coarse, fine):
            spread = [jnp.where(here, piece[r : r + 1, :], 0.0).astype(jnp.bfloat16) for r in range(ROWS)]
            total += jnp.dot(jnp.concatenate(spread, 0), hot, preferred_element_type=F32)
    for n in range(ROWS):
        forced[n] = advected[n] + total[n * LON : (n + 1) * LON]


def condense_body(place, forced, first, second, first_own, second_own, carry, ports, inner, blocks):
    even = place[0] % 2 == 0
    row = lax.broadcasted_iota(jnp.int32, (LON, LAT), 0)
    west = jnp.where(even, second[...], first[...])
    east = jnp.where(even, first[...], second[...])
    low_own = jnp.where(even, second_own[...], first_own[...])
    high_own = jnp.where(even, first_own[...], second_own[...])
    for tracer in range(TRACERS):
        full = []
        for lev in range(LEV_DEV):
            n, cx = tracer * LEV_DEV + lev, ROWS + lev
            from_west = -jnp.minimum(west[cx : cx + 1], 0.0) * (west[n : n + 1] - low_own[n : n + 1])
            from_east = jnp.maximum(high_own[cx : cx + 1], 0.0) * (east[n : n + 1] - high_own[n : n + 1])
            across = jnp.where(row == 0, from_west, jnp.where(row == LON - 1, from_east, 0.0))
            full.append(forced[n] + across)
        low = full[0]
        high = jnp.zeros((LON, LAT), F32)
        for lev in range(1, LEV_DEV):
            middle = high + full[lev]
            low = low + carry[0, lev - 1] * middle
            high = carry[1, lev - 1] * middle
            inner[tracer, lev - 1] = carry[2, lev - 1] * middle
        for w, (piece_low, piece_high) in enumerate(zip(chunks(low), chunks(high))):
            blocks[w, tracer] = piece_low
            blocks[w, TRACERS + tracer] = piece_high
    for n in range(3):
        for w, piece in enumerate(chunks(ports[n])):
            blocks[w, 2 * TRACERS + n] = piece


def chain_body(blocks, ends):
    zero = jnp.zeros((8, 128), F32)
    below, rising = [zero], [[zero] * TRACERS]
    for p in range(LEVS - 1):
        shunt, series, top = [blocks[p, 2 * TRACERS + n] for n in range(3)]
        ground = shunt + below[p]
        share = series / (series + ground)
        below.append(top + share * ground)
        rising.append([blocks[p, TRACERS + t] + share * (blocks[p, t] + rising[p][t]) for t in range(TRACERS)])
    above, sinking = zero, [zero] * TRACERS
    for p in range(LEVS - 1, -1, -1):
        shunt, series, top = [blocks[p, 2 * TRACERS + n] for n in range(3)]
        if p == LEVS - 1:
            above, sinking = shunt, [blocks[p, t] for t in range(TRACERS)]
        else:
            ground = top + above
            share = series / (series + ground)
            above = shunt + share * ground
            sinking = [blocks[p, t] + share * (blocks[p, TRACERS + t] + sinking[t]) for t in range(TRACERS)]
        inverse = 1.0 / (below[p] + above)
        for t in range(TRACERS):
            value = (rising[p][t] + sinking[t]) * inverse
            ends[p, t] = value
            if p > 0:
                ends[p - 1, TRACERS + t] = value
            if p == LEVS - 1:
                ends[p, TRACERS + t] = zero


def solve_body(inner, ends, carry, out, result, sems):
    def whole(n):
        return jnp.concatenate([jnp.concatenate([ends[2 * a, n], ends[2 * a + 1, n]], 1) for a in range(4)], 0)

    copies = []
    for tracer in range(TRACERS):
        bottom, level = whole(tracer), whole(TRACERS + tracer)
        for lev in range(LEV_DEV - 1, 0, -1):
            level = inner[tracer, lev - 1] + carry[0, lev - 1] * bottom + carry[1, lev - 1] * level
            result[tracer * LEV_DEV + lev] = level
        result[tracer * LEV_DEV] = bottom
        mine = pl.ds(tracer * LEV_DEV, LEV_DEV)
        copies.append(pltpu.make_async_copy(result.at[mine], out.at[mine], sems.at[tracer]))
        copies[-1].start()
    for copy in copies:
        copy.wait()


def per_device(adjoint, wind_x, wind_y, kz, forcing, mon_cols, mon_counts):
    place = lax.axis_index("lev").astype(jnp.int32).reshape(1)
    tile = lax.axis_index("tile").astype(jnp.int32).reshape(1)
    field = adjoint.reshape(ROWS, LON, LAT)
    inside = (LEV_DEV - 1, LON, LAT)

    payload, first_own, second_own = pack(tile, forcing, mon_cols, mon_counts, field, wind_x)
    second = lax.ppermute(second_own, "tile", [(i, (i + 1 if i % 2 else i - 1) % TILES) for i in range(TILES)])
    first = lax.ppermute(first_own, "tile", [(i, i ^ 1) for i in range(TILES)])
    received = lax.all_to_all(payload.reshape(TILES, 1, 640), "tile", 0, 0, tiled=True).reshape(TILES * 5, 128)
    carry, ports = call(block_body, ((3,) + inside, (3, LON, LAT)), [SMEM, VMEM])(place, kz)
    (advected,) = call(advect_body, ((ROWS, LON, LAT),), [VMEM] * 3, moved=2 << 20)(field, wind_x, wind_y)
    (forced,) = call(force_body, ((ROWS, LON, LAT),), [VMEM] * 2, limit=24 << 20, moved=2 << 20)(received, advected)
    inner, blocks = call(condense_body, ((TRACERS,) + inside, (LEVS, 11, 8, 128)), [SMEM] + [VMEM] * 7)(
        tile, forced, first, second, first_own, second_own, carry, ports
    )
    arrived = lax.all_to_all(blocks, "lev", 0, 0, tiled=True)
    (ends,) = call(chain_body, ((LEVS, 2 * TRACERS, 8, 128),), [VMEM])(arrived)
    ends = lax.all_to_all(ends, "lev", 0, 0, tiled=True)
    scratch = [pltpu.VMEM((ROWS, LON, LAT), F32), pltpu.SemaphoreType.DMA((TRACERS,))]
    (updated,) = call(solve_body, ((ROWS, LON, LAT),), [VMEM] * 3, scratch, out_spec=HBM)(inner, ends, carry)
    return updated.reshape(adjoint.shape)


def solution(mesh):
    in_specs = (
        P(None, "lev", "tile", None),
        P("lev", "tile", None),
        P("lev", "tile", None),
        P("lev", "tile", None),
        P("tile", None, None, "lev", None),
        P("tile", None, None),
        P("tile", None),
    )
    out_specs = P(None, "lev", "tile", None)
    return jax.shard_map(
        per_device, mesh=mesh, in_specs=in_specs, out_specs=out_specs, check_vma=False
    )
```

```python
import jax
import jax.numpy as jnp
from jax import lax
from jax.experimental import pallas as pl
from jax.experimental.pallas import tpu as pltpu
from jax.sharding import PartitionSpec as P

TRACERS = 4
LEV_DEV = 4
LEVS = 8
NLEV = 32
LON = 32
LAT = 256
TILES = 64
CAP = 32
HALF = LON // 2
ROWS = TRACERS * LEV_DEV
VMEM = pl.BlockSpec(memory_space=pltpu.VMEM)
HBM = pl.BlockSpec(memory_space=pltpu.HBM)
SMEM = pl.BlockSpec(memory_space=pltpu.SMEM)
F32 = jnp.float32


def call(body, outs, in_specs, scratch=(), limit=12 << 20, flops=0, moved=1 << 20, out_spec=VMEM, **more):
    shapes = tuple(jax.ShapeDtypeStruct(shape, F32) for shape in outs)
    return pl.pallas_call(
        body,
        out_shape=shapes,
        in_specs=in_specs,
        out_specs=out_spec if isinstance(out_spec, tuple) else (out_spec,) * len(outs),
        scratch_shapes=list(scratch),
        compiler_params=pltpu.CompilerParams(vmem_limit_bytes=limit),
        cost_estimate=pl.CostEstimate(flops=flops, bytes_accessed=moved, transcendentals=0),
        **more,
    )


def pack_body(place, force, cols, counts, adj, wind, payload, first, second, force_v, cols_v, counts_v, low_v, high_v, wind_v, message, sems):
    last = pl.ds(LON - 8, 8)
    copies = [
        pltpu.make_async_copy(force, force_v, sems.at[0]),
        pltpu.make_async_copy(cols, cols_v, sems.at[1]),
        pltpu.make_async_copy(counts, counts_v, sems.at[2]),
        pltpu.make_async_copy(adj.at[:, pl.ds(0, 8), :], low_v, sems.at[3]),
        pltpu.make_async_copy(adj.at[:, last, :], high_v, sems.at[4]),
        pltpu.make_async_copy(wind.at[:, last, :], wind_v, sems.at[5]),
    ]
    for copy in copies:
        copy.start()
    for copy in copies[:3]:
        copy.wait()
    for k in range(4):
        parts = [force_v[pl.ds(8 * k + g, ROWS, stride=CAP), :] for g in range(8)]
        message[pl.ds(k, TILES, stride=5), :] = jnp.concatenate(parts, 0).T
    slot = lax.broadcasted_iota(jnp.int32, (CAP, TILES), 0)
    lon = jnp.where(slot < counts_v[...], cols_v[...] >> 8, -1).astype(F32)
    lat = (cols_v[...] & 255).astype(F32)
    message[pl.ds(4, TILES, stride=5), :] = jnp.concatenate([lon, lat, jnp.zeros((64, TILES), F32)], 0).T
    out = pltpu.make_async_copy(message, payload, sems.at[6])
    out.start()
    for copy in copies[3:]:
        copy.wait()
    even = place[0] % 2 == 0
    low, high, cx = low_v[:, 0, :], high_v[:, 7, :], wind_v[:, 7, :]
    first[0:ROWS, :] = jnp.where(even, high, low)
    second[0:ROWS, :] = jnp.where(even, low, high)
    first[ROWS : ROWS + LEV_DEV, :] = cx
    second[ROWS : ROWS + LEV_DEV, :] = cx
    out.wait()


def pack(tile, forcing, mon_cols, mon_counts, field, wind_x):
    force = jnp.transpose(forcing[0], (1, 2, 3, 0)).reshape(ROWS * CAP, TILES)
    cols = jnp.transpose(mon_cols[0], (1, 0))
    edge = (ROWS + LEV_DEV, LAT)
    scratch = [
        pltpu.VMEM((ROWS * CAP, TILES), F32),
        pltpu.VMEM((CAP, TILES), jnp.int32),
        pltpu.VMEM((1, TILES), jnp.int32),
        pltpu.VMEM((ROWS, 8, LAT), F32),
        pltpu.VMEM((ROWS, 8, LAT), F32),
        pltpu.VMEM((LEV_DEV, 8, LAT), F32),
        pltpu.VMEM((TILES * 5, 128), F32),
        pltpu.SemaphoreType.DMA((7,)),
    ]
    operands = [pltpu.with_memory_space_constraint(x, pltpu.HBM) for x in (force, cols, mon_counts, field, wind_x)]
    return call(pack_body, ((TILES * 5, 128), edge, edge), [SMEM] + [HBM] * 5, scratch, out_spec=(HBM, VMEM, VMEM))(tile, *operands)


def prepare_body(place, adj, wind_x, wind_y, kz, out, carry, ports):
    row = lax.broadcasted_iota(jnp.int32, (LON, LAT), 0)
    lane = lax.broadcasted_iota(jnp.int32, (LON, LAT), 1)
    for lev in range(LEV_DEV):
        cx = wind_x[lev]
        cy_n = jnp.where(lane == LAT - 1, 0.0, wind_y[lev])
        cy_s = pltpu.roll(cy_n, 1, 1)
        to_east = jnp.where(row == LON - 1, 0.0, jnp.maximum(cx, 0.0))
        to_west = jnp.where(row == 0, 0.0, jnp.minimum(pltpu.roll(cx, 1, 0), 0.0))
        to_north = jnp.maximum(cy_n, 0.0)
        to_south = jnp.minimum(cy_s, 0.0)
        for tracer in range(TRACERS):
            n = tracer * LEV_DEV + lev
            a = adj[n]
            out[n] = (
                a
                + to_east * (pltpu.roll(a, LON - 1, 0) - a)
                - to_west * (pltpu.roll(a, 1, 0) - a)
                + to_north * (pltpu.roll(a, LAT - 1, 1) - a)
                - to_south * (pltpu.roll(a, 1, 1) - a)
            )
    shunt = jnp.ones((LON, LAT), F32)
    series = kz[0]
    top = jnp.zeros((LON, LAT), F32)
    for lev in range(1, LEV_DEV):
        k = kz[lev]
        if lev == LEV_DEV - 1:
            k = jnp.where(place[0] == LEVS - 1, 0.0, k)
        ground = 1.0 + top
        inverse = 1.0 / (series + k + ground)
        below, above = series * inverse, k * inverse
        carry[0, lev - 1] = below
        carry[1, lev - 1] = above
        carry[2, lev - 1] = inverse
        shunt = shunt + below * ground
        top = above * ground
        series = below * k
    ports[0] = shunt
    ports[1] = series
    ports[2] = top


def chunks(array):
    return [array[8 * (w // 2) : 8 * (w // 2) + 8, 128 * (w % 2) : 128 * (w % 2) + 128] for w in range(LEVS)]


def force_body(received, advected, forced):
    data = jnp.concatenate([received[pl.ds(k, TILES, stride=5), :] for k in range(4)], 0)
    where = received[pl.ds(4, TILES, stride=5), :]
    where = jnp.concatenate([where] + [pltpu.roll(where, 128 - 8 * k, 1) for k in range(1, 4)], 0)
    rows_all, lons = data.T, where.T
    lon_id = lax.broadcasted_iota(jnp.int32, (LON, 4 * TILES), 0).astype(F32)
    lat_id = lax.broadcasted_iota(jnp.int32, (4 * TILES, LAT), 1).astype(F32)
    total = jnp.zeros((ROWS * LON, LAT), F32)
    for g in range(8):
        here = lon_id == lons[g : g + 1, :]
        hot = jnp.where(lat_id == where[:, CAP + g : CAP + g + 1], 1.0, 0.0).astype(jnp.bfloat16)
        rows = rows_all[ROWS * g : ROWS * g + ROWS, :]
        coarse = rows.astype(jnp.bfloat16).astype(F32)
        fine = rows - coarse
        for piece in (coarse, fine):
            spread = [jnp.where(here, piece[r : r + 1, :], 0.0).astype(jnp.bfloat16) for r in range(ROWS)]
            total += jnp.dot(jnp.concatenate(spread, 0), hot, preferred_element_type=F32)
    for n in range(ROWS):
        forced[n] = advected[n] + total[n * LON : (n + 1) * LON]


def condense_body(place, forced, first, second, first_own, second_own, carry, ports, inner, blocks):
    even = place[0] % 2 == 0
    row = lax.broadcasted_iota(jnp.int32, (LON, LAT), 0)
    west = jnp.where(even, second[...], first[...])
    east = jnp.where(even, first[...], second[...])
    low_own = jnp.where(even, second_own[...], first_own[...])
    high_own = jnp.where(even, first_own[...], second_own[...])
    for tracer in range(TRACERS):
        full = []
        for lev in range(LEV_DEV):
            n, cx = tracer * LEV_DEV + lev, ROWS + lev
            from_west = -jnp.minimum(west[cx : cx + 1], 0.0) * (west[n : n + 1] - low_own[n : n + 1])
            from_east = jnp.maximum(high_own[cx : cx + 1], 0.0) * (east[n : n + 1] - high_own[n : n + 1])
            across = jnp.where(row == 0, from_west, jnp.where(row == LON - 1, from_east, 0.0))
            full.append(forced[n] + across)
        low = full[0]
        high = jnp.zeros((LON, LAT), F32)
        for lev in range(1, LEV_DEV):
            middle = high + full[lev]
            low = low + carry[0, lev - 1] * middle
            high = carry[1, lev - 1] * middle
            inner[tracer, lev - 1] = carry[2, lev - 1] * middle
        for w, (piece_low, piece_high) in enumerate(zip(chunks(low), chunks(high))):
            blocks[w, tracer] = piece_low
            blocks[w, TRACERS + tracer] = piece_high
    for n in range(3):
        for w, piece in enumerate(chunks(ports[n])):
            blocks[w, 2 * TRACERS + n] = piece


def chain_body(blocks, ends):
    zero = jnp.zeros((8, 128), F32)
    below, rising = [zero], [[zero] * TRACERS]
    for p in range(LEVS - 1):
        shunt, series, top = [blocks[p, 2 * TRACERS + n] for n in range(3)]
        ground = shunt + below[p]
        share = series / (series + ground)
        below.append(top + share * ground)
        rising.append([blocks[p, TRACERS + t] + share * (blocks[p, t] + rising[p][t]) for t in range(TRACERS)])
    above, sinking = zero, [zero] * TRACERS
    for p in range(LEVS - 1, -1, -1):
        shunt, series, top = [blocks[p, 2 * TRACERS + n] for n in range(3)]
        if p == LEVS - 1:
            above, sinking = shunt, [blocks[p, t] for t in range(TRACERS)]
        else:
            ground = top + above
            share = series / (series + ground)
            above = shunt + share * ground
            sinking = [blocks[p, t] + share * (blocks[p, TRACERS + t] + sinking[t]) for t in range(TRACERS)]
        inverse = 1.0 / (below[p] + above)
        for t in range(TRACERS):
            value = (rising[p][t] + sinking[t]) * inverse
            ends[p, t] = value
            if p > 0:
                ends[p - 1, TRACERS + t] = value
            if p == LEVS - 1:
                ends[p, TRACERS + t] = zero


def solve_body(inner, ends, carry, out, result, sems):
    def whole(n):
        return jnp.concatenate([jnp.concatenate([ends[2 * a, n], ends[2 * a + 1, n]], 1) for a in range(4)], 0)

    copies = []
    for tracer in range(TRACERS):
        bottom, level = whole(tracer), whole(TRACERS + tracer)
        for lev in range(LEV_DEV - 1, 0, -1):
            level = inner[tracer, lev - 1] + carry[0, lev - 1] * bottom + carry[1, lev - 1] * level
            result[tracer * LEV_DEV + lev] = level
        result[tracer * LEV_DEV] = bottom
        mine = pl.ds(tracer * LEV_DEV, LEV_DEV)
        copies.append(pltpu.make_async_copy(result.at[mine], out.at[mine], sems.at[tracer]))
        copies[-1].start()
    for copy in copies:
        copy.wait()


def per_device(adjoint, wind_x, wind_y, kz, forcing, mon_cols, mon_counts):
    place = lax.axis_index("lev").astype(jnp.int32).reshape(1)
    tile = lax.axis_index("tile").astype(jnp.int32).reshape(1)
    field = adjoint.reshape(ROWS, LON, LAT)
    inside = (LEV_DEV - 1, LON, LAT)

    payload, first_own, second_own = pack(tile, forcing, mon_cols, mon_counts, field, wind_x)
    second = lax.ppermute(second_own, "tile", [(i, (i + 1 if i % 2 else i - 1) % TILES) for i in range(TILES)])
    first = lax.ppermute(first_own, "tile", [(i, i ^ 1) for i in range(TILES)])
    received = lax.all_to_all(payload.reshape(TILES, 1, 640), "tile", 0, 0, tiled=True).reshape(TILES * 5, 128)
    advected, carry, ports = call(
        prepare_body,
        ((ROWS, LON, LAT), (3,) + inside, (3, LON, LAT)),
        [SMEM] + [VMEM] * 4,
        moved=2 << 20,
    )(place, field, wind_x, wind_y, kz)
    (forced,) = call(force_body, ((ROWS, LON, LAT),), [VMEM] * 2, limit=24 << 20, moved=2 << 20)(received, advected)
    inner, blocks = call(condense_body, ((TRACERS,) + inside, (LEVS, 11, 8, 128)), [SMEM] + [VMEM] * 7)(
        tile, forced, first, second, first_own, second_own, carry, ports
    )
    arrived = lax.all_to_all(blocks, "lev", 0, 0, tiled=True)
    (ends,) = call(chain_body, ((LEVS, 2 * TRACERS, 8, 128),), [VMEM])(arrived)
    ends = lax.all_to_all(ends, "lev", 0, 0, tiled=True)
    scratch = [pltpu.VMEM((ROWS, LON, LAT), F32), pltpu.SemaphoreType.DMA((TRACERS,))]
    (updated,) = call(solve_body, ((ROWS, LON, LAT),), [VMEM] * 3, scratch, out_spec=HBM)(inner, ends, carry)
    return updated.reshape(adjoint.shape)


def solution(mesh):
    in_specs = (
        P(None, "lev", "tile", None),
        P("lev", "tile", None),
        P("lev", "tile", None),
        P("lev", "tile", None),
        P("tile", None, None, "lev", None),
        P("tile", None, None),
        P("tile", None),
    )
    out_specs = P(None, "lev", "tile", None)
    return jax.shard_map(
        per_device, mesh=mesh, in_specs=in_specs, out_specs=out_specs, check_vma=False
    )
```

```python
import jax
import jax.numpy as jnp
from jax import lax
from jax.experimental import pallas as pl
from jax.experimental.pallas import tpu as pltpu
from jax.sharding import PartitionSpec as P

TRACERS = 4
LEV_DEV = 4
LEVS = 8
NLEV = 32
LON = 32
LAT = 256
TILES = 64
CAP = 32
HALF = LON // 2
ROWS = TRACERS * LEV_DEV
VMEM = pl.BlockSpec(memory_space=pltpu.VMEM)
HBM = pl.BlockSpec(memory_space=pltpu.HBM)
SMEM = pl.BlockSpec(memory_space=pltpu.SMEM)
F32 = jnp.float32


def call(body, outs, in_specs, scratch=(), limit=12 << 20, flops=0, moved=1 << 20, out_spec=VMEM, **more):
    shapes = tuple(jax.ShapeDtypeStruct(shape, F32) for shape in outs)
    return pl.pallas_call(
        body,
        out_shape=shapes,
        in_specs=in_specs,
        out_specs=out_spec if isinstance(out_spec, tuple) else (out_spec,) * len(outs),
        scratch_shapes=list(scratch),
        compiler_params=pltpu.CompilerParams(vmem_limit_bytes=limit),
        cost_estimate=pl.CostEstimate(flops=flops, bytes_accessed=moved, transcendentals=0),
        **more,
    )


def pack_body(
    tile, place, force, cols, counts, adj, wind, wind_y, kz, payload, first, second, advected, carry, ports,
    force_v, cols_v, counts_v, adj_v, wind_v, wind_y_v, kz_v, message, sems,
):
    copies = [
        pltpu.make_async_copy(force, force_v, sems.at[0]),
        pltpu.make_async_copy(cols, cols_v, sems.at[1]),
        pltpu.make_async_copy(counts, counts_v, sems.at[2]),
        pltpu.make_async_copy(adj, adj_v, sems.at[3]),
        pltpu.make_async_copy(wind, wind_v, sems.at[4]),
        pltpu.make_async_copy(wind_y, wind_y_v, sems.at[5]),
        pltpu.make_async_copy(kz, kz_v, sems.at[7]),
    ]
    for copy in copies:
        copy.start()
    for copy in copies[:3]:
        copy.wait()
    for k in range(4):
        parts = [force_v[pl.ds(8 * k + g, ROWS, stride=CAP), :] for g in range(8)]
        message[pl.ds(k, TILES, stride=5), :] = jnp.concatenate(parts, 0).T
    slot = lax.broadcasted_iota(jnp.int32, (CAP, TILES), 0)
    lon = jnp.where(slot < counts_v[...], cols_v[...] >> 8, -1).astype(F32)
    lat = (cols_v[...] & 255).astype(F32)
    message[pl.ds(4, TILES, stride=5), :] = jnp.concatenate([lon, lat, jnp.zeros((64, TILES), F32)], 0).T
    out = pltpu.make_async_copy(message, payload, sems.at[6])
    out.start()
    for copy in copies[3:]:
        copy.wait()
    even = tile[0] % 2 == 0
    low, high, cx = adj_v[:, 0, :], adj_v[:, LON - 1, :], wind_v[:, LON - 1, :]
    first[0:ROWS, :] = jnp.where(even, high, low)
    second[0:ROWS, :] = jnp.where(even, low, high)
    first[ROWS : ROWS + LEV_DEV, :] = cx
    second[ROWS : ROWS + LEV_DEV, :] = cx
    prepare_body(place, adj_v, wind_v, wind_y_v, kz_v, advected, carry, ports)
    out.wait()


def pack(tile, place, forcing, mon_cols, mon_counts, field, wind_x, wind_y, kz):
    force = jnp.transpose(forcing[0], (1, 2, 3, 0)).reshape(ROWS * CAP, TILES)
    cols = jnp.transpose(mon_cols[0], (1, 0))
    edge = (ROWS + LEV_DEV, LAT)
    scratch = [
        pltpu.VMEM((ROWS * CAP, TILES), F32),
        pltpu.VMEM((CAP, TILES), jnp.int32),
        pltpu.VMEM((1, TILES), jnp.int32),
        pltpu.VMEM((ROWS, LON, LAT), F32),
        pltpu.VMEM((LEV_DEV, LON, LAT), F32),
        pltpu.VMEM((LEV_DEV, LON, LAT), F32),
        pltpu.VMEM((LEV_DEV, LON, LAT), F32),
        pltpu.VMEM((TILES * 5, 128), F32),
        pltpu.SemaphoreType.DMA((8,)),
    ]
    operands = [pltpu.with_memory_space_constraint(x, pltpu.HBM) for x in (force, cols, mon_counts, field, wind_x, wind_y, kz)]
    outs = ((TILES * 5, 128), edge, edge, (ROWS, LON, LAT), (3, LEV_DEV - 1, LON, LAT), (3, LON, LAT))
    specs = [SMEM] * 2 + [HBM] * 7
    return call(pack_body, outs, specs, scratch, out_spec=(HBM,) + (VMEM,) * 5)(tile, place, *operands)


def prepare_body(place, adj, wind_x, wind_y, kz, out, carry, ports):
    row = lax.broadcasted_iota(jnp.int32, (LON, LAT), 0)
    lane = lax.broadcasted_iota(jnp.int32, (LON, LAT), 1)
    for lev in range(LEV_DEV):
        cx = wind_x[lev]
        cy_n = jnp.where(lane == LAT - 1, 0.0, wind_y[lev])
        cy_s = pltpu.roll(cy_n, 1, 1)
        to_east = jnp.where(row == LON - 1, 0.0, jnp.maximum(cx, 0.0))
        to_west = jnp.where(row == 0, 0.0, jnp.minimum(pltpu.roll(cx, 1, 0), 0.0))
        to_north = jnp.maximum(cy_n, 0.0)
        to_south = jnp.minimum(cy_s, 0.0)
        for tracer in range(TRACERS):
            n = tracer * LEV_DEV + lev
            a = adj[n]
            out[n] = (
                a
                + to_east * (pltpu.roll(a, LON - 1, 0) - a)
                - to_west * (pltpu.roll(a, 1, 0) - a)
                + to_north * (pltpu.roll(a, LAT - 1, 1) - a)
                - to_south * (pltpu.roll(a, 1, 1) - a)
            )
    shunt = jnp.ones((LON, LAT), F32)
    series = kz[0]
    top = jnp.zeros((LON, LAT), F32)
    for lev in range(1, LEV_DEV):
        k = kz[lev]
        if lev == LEV_DEV - 1:
            k = jnp.where(place[0] == LEVS - 1, 0.0, k)
        ground = 1.0 + top
        inverse = 1.0 / (series + k + ground)
        below, above = series * inverse, k * inverse
        carry[0, lev - 1] = below
        carry[1, lev - 1] = above
        carry[2, lev - 1] = inverse
        shunt = shunt + below * ground
        top = above * ground
        series = below * k
    ports[0] = shunt
    ports[1] = series
    ports[2] = top


def chunks(array):
    return [array[8 * (w // 2) : 8 * (w // 2) + 8, 128 * (w % 2) : 128 * (w % 2) + 128] for w in range(LEVS)]


def force_body(received, advected, forced):
    data = jnp.concatenate([received[pl.ds(k, TILES, stride=5), :] for k in range(4)], 0)
    where = received[pl.ds(4, TILES, stride=5), :]
    where = jnp.concatenate([where] + [pltpu.roll(where, 128 - 8 * k, 1) for k in range(1, 4)], 0)
    rows_all, lons = data.T, where.T
    lon_id = lax.broadcasted_iota(jnp.int32, (LON, 4 * TILES), 0).astype(F32)
    lat_id = lax.broadcasted_iota(jnp.int32, (4 * TILES, LAT), 1).astype(F32)
    total = jnp.zeros((ROWS * LON, LAT), F32)
    for g in range(8):
        here = lon_id == lons[g : g + 1, :]
        hot = jnp.where(lat_id == where[:, CAP + g : CAP + g + 1], 1.0, 0.0).astype(jnp.bfloat16)
        rows = rows_all[ROWS * g : ROWS * g + ROWS, :]
        coarse = rows.astype(jnp.bfloat16).astype(F32)
        fine = rows - coarse
        for piece in (coarse, fine):
            spread = [jnp.where(here, piece[r : r + 1, :], 0.0).astype(jnp.bfloat16) for r in range(ROWS)]
            total += jnp.dot(jnp.concatenate(spread, 0), hot, preferred_element_type=F32)
    for n in range(ROWS):
        forced[n] = advected[n] + total[n * LON : (n + 1) * LON]


def condense_body(place, forced, first, second, first_own, second_own, carry, ports, inner, blocks):
    even = place[0] % 2 == 0
    row = lax.broadcasted_iota(jnp.int32, (LON, LAT), 0)
    west = jnp.where(even, second[...], first[...])
    east = jnp.where(even, first[...], second[...])
    low_own = jnp.where(even, second_own[...], first_own[...])
    high_own = jnp.where(even, first_own[...], second_own[...])
    for tracer in range(TRACERS):
        full = []
        for lev in range(LEV_DEV):
            n, cx = tracer * LEV_DEV + lev, ROWS + lev
            from_west = -jnp.minimum(west[cx : cx + 1], 0.0) * (west[n : n + 1] - low_own[n : n + 1])
            from_east = jnp.maximum(high_own[cx : cx + 1], 0.0) * (east[n : n + 1] - high_own[n : n + 1])
            across = jnp.where(row == 0, from_west, jnp.where(row == LON - 1, from_east, 0.0))
            full.append(forced[n] + across)
        low = full[0]
        high = jnp.zeros((LON, LAT), F32)
        for lev in range(1, LEV_DEV):
            middle = high + full[lev]
            low = low + carry[0, lev - 1] * middle
            high = carry[1, lev - 1] * middle
            inner[tracer, lev - 1] = carry[2, lev - 1] * middle
        for w, (piece_low, piece_high) in enumerate(zip(chunks(low), chunks(high))):
            blocks[w, tracer] = piece_low
            blocks[w, TRACERS + tracer] = piece_high
    for n in range(3):
        for w, piece in enumerate(chunks(ports[n])):
            blocks[w, 2 * TRACERS + n] = piece


def chain_body(blocks, ends):
    zero = jnp.zeros((8, 128), F32)
    below, rising = [zero], [[zero] * TRACERS]
    for p in range(LEVS - 1):
        shunt, series, top = [blocks[p, 2 * TRACERS + n] for n in range(3)]
        ground = shunt + below[p]
        share = series / (series + ground)
        below.append(top + share * ground)
        rising.append([blocks[p, TRACERS + t] + share * (blocks[p, t] + rising[p][t]) for t in range(TRACERS)])
    above, sinking = zero, [zero] * TRACERS
    for p in range(LEVS - 1, -1, -1):
        shunt, series, top = [blocks[p, 2 * TRACERS + n] for n in range(3)]
        if p == LEVS - 1:
            above, sinking = shunt, [blocks[p, t] for t in range(TRACERS)]
        else:
            ground = top + above
            share = series / (series + ground)
            above = shunt + share * ground
            sinking = [blocks[p, t] + share * (blocks[p, TRACERS + t] + sinking[t]) for t in range(TRACERS)]
        inverse = 1.0 / (below[p] + above)
        for t in range(TRACERS):
            value = (rising[p][t] + sinking[t]) * inverse
            ends[p, t] = value
            if p > 0:
                ends[p - 1, TRACERS + t] = value
            if p == LEVS - 1:
                ends[p, TRACERS + t] = zero


def solve_body(inner, ends, carry, out, result, sems):
    def whole(n):
        return jnp.concatenate([jnp.concatenate([ends[2 * a, n], ends[2 * a + 1, n]], 1) for a in range(4)], 0)

    copies = []
    for tracer in range(TRACERS):
        bottom, level = whole(tracer), whole(TRACERS + tracer)
        for lev in range(LEV_DEV - 1, 0, -1):
            level = inner[tracer, lev - 1] + carry[0, lev - 1] * bottom + carry[1, lev - 1] * level
            result[tracer * LEV_DEV + lev] = level
        result[tracer * LEV_DEV] = bottom
        mine = pl.ds(tracer * LEV_DEV, LEV_DEV)
        copies.append(pltpu.make_async_copy(result.at[mine], out.at[mine], sems.at[tracer]))
        copies[-1].start()
    for copy in copies:
        copy.wait()


def per_device(adjoint, wind_x, wind_y, kz, forcing, mon_cols, mon_counts):
    place = lax.axis_index("lev").astype(jnp.int32).reshape(1)
    tile = lax.axis_index("tile").astype(jnp.int32).reshape(1)
    field = adjoint.reshape(ROWS, LON, LAT)
    inside = (LEV_DEV - 1, LON, LAT)

    payload, first_own, second_own, advected, carry, ports = pack(
        tile, place, forcing, mon_cols, mon_counts, field, wind_x, wind_y, kz
    )
    second = lax.ppermute(second_own, "tile", [(i, (i + 1 if i % 2 else i - 1) % TILES) for i in range(TILES)])
    first = lax.ppermute(first_own, "tile", [(i, i ^ 1) for i in range(TILES)])
    received = lax.all_to_all(payload.reshape(TILES, 1, 640), "tile", 0, 0, tiled=True).reshape(TILES * 5, 128)
    (forced,) = call(force_body, ((ROWS, LON, LAT),), [VMEM] * 2, limit=24 << 20, moved=2 << 20)(received, advected)
    inner, blocks = call(condense_body, ((TRACERS,) + inside, (LEVS, 11, 8, 128)), [SMEM] + [VMEM] * 7)(
        tile, forced, first, second, first_own, second_own, carry, ports
    )
    arrived = lax.all_to_all(blocks, "lev", 0, 0, tiled=True)
    (ends,) = call(chain_body, ((LEVS, 2 * TRACERS, 8, 128),), [VMEM])(arrived)
    ends = lax.all_to_all(ends, "lev", 0, 0, tiled=True)
    scratch = [pltpu.VMEM((ROWS, LON, LAT), F32), pltpu.SemaphoreType.DMA((TRACERS,))]
    (updated,) = call(solve_body, ((ROWS, LON, LAT),), [VMEM] * 3, scratch, out_spec=HBM)(inner, ends, carry)
    return updated.reshape(adjoint.shape)


def solution(mesh):
    in_specs = (
        P(None, "lev", "tile", None),
        P("lev", "tile", None),
        P("lev", "tile", None),
        P("lev", "tile", None),
        P("tile", None, None, "lev", None),
        P("tile", None, None),
        P("tile", None),
    )
    out_specs = P(None, "lev", "tile", None)
    return jax.shard_map(
        per_device, mesh=mesh, in_specs=in_specs, out_specs=out_specs, check_vma=False
    )
```

```python
import jax
import jax.numpy as jnp
from jax import lax
from jax.experimental import pallas as pl
from jax.experimental.pallas import tpu as pltpu
from jax.sharding import PartitionSpec as P

TRACERS = 4
LEV_DEV = 4
LEVS = 8
NLEV = 32
LON = 32
LAT = 256
TILES = 64
CAP = 32
HALF = LON // 2
ROWS = TRACERS * LEV_DEV
VMEM = pl.BlockSpec(memory_space=pltpu.VMEM)
HBM = pl.BlockSpec(memory_space=pltpu.HBM)
SMEM = pl.BlockSpec(memory_space=pltpu.SMEM)
F32 = jnp.float32


def call(body, outs, in_specs, scratch=(), limit=12 << 20, flops=0, moved=1 << 20, out_spec=VMEM, **more):
    shapes = tuple(jax.ShapeDtypeStruct(shape, F32) for shape in outs)
    return pl.pallas_call(
        body,
        out_shape=shapes,
        in_specs=in_specs,
        out_specs=out_spec if isinstance(out_spec, tuple) else (out_spec,) * len(outs),
        scratch_shapes=list(scratch),
        compiler_params=pltpu.CompilerParams(vmem_limit_bytes=limit),
        cost_estimate=pl.CostEstimate(flops=flops, bytes_accessed=moved, transcendentals=0),
        **more,
    )


def pack_body(
    tile, place, force, cols, counts, adj, wind, wind_y, kz, payload, first, second, advected, carry, ports,
    force_v, cols_v, counts_v, adj_v, wind_v, wind_y_v, kz_v, message, sems,
):
    copies = [
        pltpu.make_async_copy(force, force_v, sems.at[0]),
        pltpu.make_async_copy(cols, cols_v, sems.at[1]),
        pltpu.make_async_copy(counts, counts_v, sems.at[2]),
        pltpu.make_async_copy(adj, adj_v, sems.at[3]),
        pltpu.make_async_copy(wind, wind_v, sems.at[4]),
        pltpu.make_async_copy(wind_y, wind_y_v, sems.at[5]),
        pltpu.make_async_copy(kz, kz_v, sems.at[7]),
    ]
    for copy in copies:
        copy.start()
    for copy in copies[:3]:
        copy.wait()
    for k in range(4):
        parts = [force_v[pl.ds(8 * k + g, ROWS, stride=CAP), :] for g in range(8)]
        message[pl.ds(k, TILES, stride=5), :] = jnp.concatenate(parts, 0).T
    slot = lax.broadcasted_iota(jnp.int32, (CAP, TILES), 0)
    lon = jnp.where(slot < counts_v[...], cols_v[...] >> 8, -1).astype(F32)
    lat = (cols_v[...] & 255).astype(F32)
    message[pl.ds(4, TILES, stride=5), :] = jnp.concatenate([lon, lat, jnp.zeros((64, TILES), F32)], 0).T
    out = pltpu.make_async_copy(message, payload, sems.at[6])
    out.start()
    for copy in copies[3:]:
        copy.wait()
    even = tile[0] % 2 == 0
    low, high, cx = adj_v[:, 0, :], adj_v[:, LON - 1, :], wind_v[:, LON - 1, :]
    first[0:ROWS, :] = jnp.where(even, high, low)
    second[0:ROWS, :] = jnp.where(even, low, high)
    first[ROWS : ROWS + LEV_DEV, :] = cx
    second[ROWS : ROWS + LEV_DEV, :] = cx
    prepare_body(place, adj_v, wind_v, wind_y_v, kz_v, advected, carry, ports)
    out.wait()


def pack(tile, place, forcing, mon_cols, mon_counts, field, wind_x, wind_y, kz):
    force = jnp.transpose(forcing[0], (1, 2, 3, 0)).reshape(ROWS * CAP, TILES)
    cols = jnp.transpose(mon_cols[0], (1, 0))
    edge = (ROWS + LEV_DEV, LAT)
    scratch = [
        pltpu.VMEM((ROWS * CAP, TILES), F32),
        pltpu.VMEM((CAP, TILES), jnp.int32),
        pltpu.VMEM((1, TILES), jnp.int32),
        pltpu.VMEM((ROWS, LON, LAT), F32),
        pltpu.VMEM((LEV_DEV, LON, LAT), F32),
        pltpu.VMEM((LEV_DEV, LON, LAT), F32),
        pltpu.VMEM((LEV_DEV, LON, LAT), F32),
        pltpu.VMEM((TILES * 5, 128), F32),
        pltpu.SemaphoreType.DMA((8,)),
    ]
    operands = [pltpu.with_memory_space_constraint(x, pltpu.HBM) for x in (force, cols, mon_counts, field, wind_x, wind_y, kz)]
    outs = ((TILES * 5, 128), edge, edge, (ROWS, LON, LAT), (3, LEV_DEV - 1, LON, LAT), (3, LON, LAT))
    specs = [SMEM] * 2 + [HBM] * 7
    return call(pack_body, outs, specs, scratch, out_spec=(HBM,) + (VMEM,) * 5)(tile, place, *operands)


def prepare_body(place, adj, wind_x, wind_y, kz, out, carry, ports):
    row = lax.broadcasted_iota(jnp.int32, (LON, LAT), 0)
    lane = lax.broadcasted_iota(jnp.int32, (LON, LAT), 1)
    for lev in range(LEV_DEV):
        cx = wind_x[lev]
        cy_n = jnp.where(lane == LAT - 1, 0.0, wind_y[lev])
        cy_s = pltpu.roll(cy_n, 1, 1)
        to_east = jnp.where(row == LON - 1, 0.0, jnp.maximum(cx, 0.0))
        to_west = jnp.where(row == 0, 0.0, jnp.minimum(pltpu.roll(cx, 1, 0), 0.0))
        to_north = jnp.maximum(cy_n, 0.0)
        to_south = jnp.minimum(cy_s, 0.0)
        for tracer in range(TRACERS):
            n = tracer * LEV_DEV + lev
            a = adj[n]
            out[n] = (
                a
                + to_east * (pltpu.roll(a, LON - 1, 0) - a)
                - to_west * (pltpu.roll(a, 1, 0) - a)
                + to_north * (pltpu.roll(a, LAT - 1, 1) - a)
                - to_south * (pltpu.roll(a, 1, 1) - a)
            )
    shunt = jnp.ones((LON, LAT), F32)
    series = kz[0]
    top = jnp.zeros((LON, LAT), F32)
    for lev in range(1, LEV_DEV):
        k = kz[lev]
        if lev == LEV_DEV - 1:
            k = jnp.where(place[0] == LEVS - 1, 0.0, k)
        ground = 1.0 + top
        inverse = 1.0 / (series + k + ground)
        below, above = series * inverse, k * inverse
        carry[0, lev - 1] = below
        carry[1, lev - 1] = above
        carry[2, lev - 1] = inverse
        shunt = shunt + below * ground
        top = above * ground
        series = below * k
    ports[0] = shunt
    ports[1] = series
    ports[2] = top


def chunks(array):
    return [array[8 * (w // 2) : 8 * (w // 2) + 8, 128 * (w % 2) : 128 * (w % 2) + 128] for w in range(LEVS)]


def pass_body(near, out):
    out[...] = near[...]


def force_body(received, advected, forced):
    data = jnp.concatenate([received[pl.ds(k, TILES, stride=5), :] for k in range(4)], 0)
    where = received[pl.ds(4, TILES, stride=5), :]
    where = jnp.concatenate([where] + [pltpu.roll(where, 128 - 8 * k, 1) for k in range(1, 4)], 0)
    rows_all, lons = data.T, where.T
    lon_id = lax.broadcasted_iota(jnp.int32, (LON, 4 * TILES), 0).astype(F32)
    lat_id = lax.broadcasted_iota(jnp.int32, (4 * TILES, LAT), 1).astype(F32)
    total = jnp.zeros((ROWS * LON, LAT), F32)
    for g in range(8):
        here = lon_id == lons[g : g + 1, :]
        hot = jnp.where(lat_id == where[:, CAP + g : CAP + g + 1], 1.0, 0.0).astype(jnp.bfloat16)
        rows = rows_all[ROWS * g : ROWS * g + ROWS, :]
        coarse = rows.astype(jnp.bfloat16).astype(F32)
        fine = rows - coarse
        for piece in (coarse, fine):
            spread = [jnp.where(here, piece[r : r + 1, :], 0.0).astype(jnp.bfloat16) for r in range(ROWS)]
            total += jnp.dot(jnp.concatenate(spread, 0), hot, preferred_element_type=F32)
    for n in range(ROWS):
        forced[n] = advected[n] + total[n * LON : (n + 1) * LON]


def condense_body(place, forced, first, second, first_own, second_own, carry, ports, inner, blocks):
    even = place[0] % 2 == 0
    row = lax.broadcasted_iota(jnp.int32, (LON, LAT), 0)
    west = jnp.where(even, second[...], first[...])
    east = jnp.where(even, first[...], second[...])
    low_own = jnp.where(even, second_own[...], first_own[...])
    high_own = jnp.where(even, first_own[...], second_own[...])
    for tracer in range(TRACERS):
        full = []
        for lev in range(LEV_DEV):
            n, cx = tracer * LEV_DEV + lev, ROWS + lev
            from_west = -jnp.minimum(west[cx : cx + 1], 0.0) * (west[n : n + 1] - low_own[n : n + 1])
            from_east = jnp.maximum(high_own[cx : cx + 1], 0.0) * (east[n : n + 1] - high_own[n : n + 1])
            across = jnp.where(row == 0, from_west, jnp.where(row == LON - 1, from_east, 0.0))
            full.append(forced[n] + across)
        low = full[0]
        high = jnp.zeros((LON, LAT), F32)
        for lev in range(1, LEV_DEV):
            middle = high + full[lev]
            low = low + carry[0, lev - 1] * middle
            high = carry[1, lev - 1] * middle
            inner[tracer, lev - 1] = carry[2, lev - 1] * middle
        for w, (piece_low, piece_high) in enumerate(zip(chunks(low), chunks(high))):
            blocks[w, tracer] = piece_low
            blocks[w, TRACERS + tracer] = piece_high
    for n in range(3):
        for w, piece in enumerate(chunks(ports[n])):
            blocks[w, 2 * TRACERS + n] = piece


def chain_body(blocks, ends):
    zero = jnp.zeros((8, 128), F32)
    below, rising = [zero], [[zero] * TRACERS]
    for p in range(LEVS - 1):
        shunt, series, top = [blocks[p, 2 * TRACERS + n] for n in range(3)]
        ground = shunt + below[p]
        share = series / (series + ground)
        below.append(top + share * ground)
        rising.append([blocks[p, TRACERS + t] + share * (blocks[p, t] + rising[p][t]) for t in range(TRACERS)])
    above, sinking = zero, [zero] * TRACERS
    for p in range(LEVS - 1, -1, -1):
        shunt, series, top = [blocks[p, 2 * TRACERS + n] for n in range(3)]
        if p == LEVS - 1:
            above, sinking = shunt, [blocks[p, t] for t in range(TRACERS)]
        else:
            ground = top + above
            share = series / (series + ground)
            above = shunt + share * ground
            sinking = [blocks[p, t] + share * (blocks[p, TRACERS + t] + sinking[t]) for t in range(TRACERS)]
        inverse = 1.0 / (below[p] + above)
        for t in range(TRACERS):
            value = (rising[p][t] + sinking[t]) * inverse
            ends[p, t] = value
            if p > 0:
                ends[p - 1, TRACERS + t] = value
            if p == LEVS - 1:
                ends[p, TRACERS + t] = zero


def solve_body(inner, ends, carry, out, result, sems):
    def whole(n):
        return jnp.concatenate([jnp.concatenate([ends[2 * a, n], ends[2 * a + 1, n]], 1) for a in range(4)], 0)

    copies = []
    for tracer in range(TRACERS):
        bottom, level = whole(tracer), whole(TRACERS + tracer)
        for lev in range(LEV_DEV - 1, 0, -1):
            level = inner[tracer, lev - 1] + carry[0, lev - 1] * bottom + carry[1, lev - 1] * level
            result[tracer * LEV_DEV + lev] = level
        result[tracer * LEV_DEV] = bottom
        mine = pl.ds(tracer * LEV_DEV, LEV_DEV)
        copies.append(pltpu.make_async_copy(result.at[mine], out.at[mine], sems.at[tracer]))
        copies[-1].start()
    for copy in copies:
        copy.wait()


def per_device(adjoint, wind_x, wind_y, kz, forcing, mon_cols, mon_counts):
    place = lax.axis_index("lev").astype(jnp.int32).reshape(1)
    tile = lax.axis_index("tile").astype(jnp.int32).reshape(1)
    field = adjoint.reshape(ROWS, LON, LAT)
    inside = (LEV_DEV - 1, LON, LAT)

    payload, first_own, second_own, advected, carry, ports = pack(
        tile, place, forcing, mon_cols, mon_counts, field, wind_x, wind_y, kz
    )
    second = lax.ppermute(second_own, "tile", [(i, (i + 1 if i % 2 else i - 1) % TILES) for i in range(TILES)])
    (near,) = call(pass_body, (first_own.shape,), [VMEM])(first_own)
    first = lax.ppermute(near, "tile", [(i, i ^ 1) for i in range(TILES)])
    received = lax.all_to_all(payload.reshape(TILES, 1, 640), "tile", 0, 0, tiled=True).reshape(TILES * 5, 128)
    (forced,) = call(force_body, ((ROWS, LON, LAT),), [VMEM] * 2, limit=24 << 20, moved=2 << 20)(received, advected)
    inner, blocks = call(condense_body, ((TRACERS,) + inside, (LEVS, 11, 8, 128)), [SMEM] + [VMEM] * 7)(
        tile, forced, first, second, first_own, second_own, carry, ports
    )
    arrived = lax.all_to_all(blocks, "lev", 0, 0, tiled=True)
    (ends,) = call(chain_body, ((LEVS, 2 * TRACERS, 8, 128),), [VMEM])(arrived)
    ends = lax.all_to_all(ends, "lev", 0, 0, tiled=True)
    scratch = [pltpu.VMEM((ROWS, LON, LAT), F32), pltpu.SemaphoreType.DMA((TRACERS,))]
    (updated,) = call(solve_body, ((ROWS, LON, LAT),), [VMEM] * 3, scratch, out_spec=HBM)(inner, ends, carry)
    return updated.reshape(adjoint.shape)


def solution(mesh):
    in_specs = (
        P(None, "lev", "tile", None),
        P("lev", "tile", None),
        P("lev", "tile", None),
        P("lev", "tile", None),
        P("tile", None, None, "lev", None),
        P("tile", None, None),
        P("tile", None),
    )
    out_specs = P(None, "lev", "tile", None)
    return jax.shard_map(
        per_device, mesh=mesh, in_specs=in_specs, out_specs=out_specs, check_vma=False
    )
```

```python
import jax
import jax.numpy as jnp
from jax import lax
from jax.experimental import pallas as pl
from jax.experimental.pallas import tpu as pltpu
from jax.sharding import PartitionSpec as P

TRACERS = 4
LEV_DEV = 4
LEVS = 8
NLEV = 32
LON = 32
LAT = 256
TILES = 64
CAP = 32
HALF = LON // 2
ROWS = TRACERS * LEV_DEV
VMEM = pl.BlockSpec(memory_space=pltpu.VMEM)
HBM = pl.BlockSpec(memory_space=pltpu.HBM)
SMEM = pl.BlockSpec(memory_space=pltpu.SMEM)
F32 = jnp.float32


def call(body, outs, in_specs, scratch=(), limit=12 << 20, flops=0, moved=1 << 20, out_spec=VMEM, **more):
    shapes = tuple(jax.ShapeDtypeStruct(shape, F32) for shape in outs)
    return pl.pallas_call(
        body,
        out_shape=shapes,
        in_specs=in_specs,
        out_specs=out_spec if isinstance(out_spec, tuple) else (out_spec,) * len(outs),
        scratch_shapes=list(scratch),
        compiler_params=pltpu.CompilerParams(vmem_limit_bytes=limit),
        cost_estimate=pl.CostEstimate(flops=flops, bytes_accessed=moved, transcendentals=0),
        **more,
    )


def pack_body(
    tile, place, force, cols, counts, adj, wind, wind_y, kz, payload, first, second, advected, carry, ports,
    force_v, cols_v, counts_v, adj_v, wind_v, wind_y_v, kz_v, message, sems,
):
    copies = [
        pltpu.make_async_copy(force, force_v, sems.at[0]),
        pltpu.make_async_copy(cols, cols_v, sems.at[1]),
        pltpu.make_async_copy(counts, counts_v, sems.at[2]),
        pltpu.make_async_copy(adj, adj_v, sems.at[3]),
        pltpu.make_async_copy(wind, wind_v, sems.at[4]),
        pltpu.make_async_copy(wind_y, wind_y_v, sems.at[5]),
        pltpu.make_async_copy(kz, kz_v, sems.at[7]),
    ]
    for copy in copies:
        copy.start()
    for copy in copies[:3]:
        copy.wait()
    for k in range(4):
        parts = [force_v[pl.ds(8 * k + g, ROWS, stride=CAP), :] for g in range(8)]
        message[pl.ds(k, TILES, stride=5), :] = jnp.concatenate(parts, 0).T
    slot = lax.broadcasted_iota(jnp.int32, (CAP, TILES), 0)
    lon = jnp.where(slot < counts_v[...], cols_v[...] >> 8, -1).astype(F32)
    lat = (cols_v[...] & 255).astype(F32)
    message[pl.ds(4, TILES, stride=5), :] = jnp.concatenate([lon, lat, jnp.zeros((64, TILES), F32)], 0).T
    out = pltpu.make_async_copy(message, payload, sems.at[6])
    out.start()
    for copy in copies[3:]:
        copy.wait()
    even = tile[0] % 2 == 0
    low, high, cx = adj_v[:, 0, :], adj_v[:, LON - 1, :], wind_v[:, LON - 1, :]
    first[0:ROWS, :] = jnp.where(even, high, low)
    second[0:ROWS, :] = jnp.where(even, low, high)
    first[ROWS : ROWS + LEV_DEV, :] = cx
    second[ROWS : ROWS + LEV_DEV, :] = cx
    prepare_body(place, adj_v, wind_v, wind_y_v, kz_v, advected, carry, ports)
    out.wait()


def pack(tile, place, forcing, mon_cols, mon_counts, field, wind_x, wind_y, kz):
    force = jnp.transpose(forcing[0], (1, 2, 3, 0)).reshape(ROWS * CAP, TILES)
    cols = jnp.transpose(mon_cols[0], (1, 0))
    edge = (ROWS + LEV_DEV, LAT)
    scratch = [
        pltpu.VMEM((ROWS * CAP, TILES), F32),
        pltpu.VMEM((CAP, TILES), jnp.int32),
        pltpu.VMEM((1, TILES), jnp.int32),
        pltpu.VMEM((ROWS, LON, LAT), F32),
        pltpu.VMEM((LEV_DEV, LON, LAT), F32),
        pltpu.VMEM((LEV_DEV, LON, LAT), F32),
        pltpu.VMEM((LEV_DEV, LON, LAT), F32),
        pltpu.VMEM((TILES * 5, 128), F32),
        pltpu.SemaphoreType.DMA((8,)),
    ]
    operands = [pltpu.with_memory_space_constraint(x, pltpu.HBM) for x in (force, cols, mon_counts, field, wind_x, wind_y, kz)]
    outs = ((TILES * 5, 128), edge, edge, (ROWS, LON, LAT), (3, LEV_DEV - 1, LON, LAT), (3, LON, LAT))
    specs = [SMEM] * 2 + [HBM] * 7
    return call(pack_body, outs, specs, scratch, out_spec=(HBM,) + (VMEM,) * 5)(tile, place, *operands)


def prepare_body(place, adj, wind_x, wind_y, kz, out, carry, ports):
    row = lax.broadcasted_iota(jnp.int32, (LON, LAT), 0)
    lane = lax.broadcasted_iota(jnp.int32, (LON, LAT), 1)
    for lev in range(LEV_DEV):
        cx = wind_x[lev]
        cy_n = jnp.where(lane == LAT - 1, 0.0, wind_y[lev])
        cy_s = pltpu.roll(cy_n, 1, 1)
        to_east = jnp.where(row == LON - 1, 0.0, jnp.maximum(cx, 0.0))
        to_west = jnp.where(row == 0, 0.0, jnp.minimum(pltpu.roll(cx, 1, 0), 0.0))
        to_north = jnp.maximum(cy_n, 0.0)
        to_south = jnp.minimum(cy_s, 0.0)
        for tracer in range(TRACERS):
            n = tracer * LEV_DEV + lev
            a = adj[n]
            out[n] = (
                a
                + to_east * (pltpu.roll(a, LON - 1, 0) - a)
                - to_west * (pltpu.roll(a, 1, 0) - a)
                + to_north * (pltpu.roll(a, LAT - 1, 1) - a)
                - to_south * (pltpu.roll(a, 1, 1) - a)
            )
    shunt = jnp.ones((LON, LAT), F32)
    series = kz[0]
    top = jnp.zeros((LON, LAT), F32)
    for lev in range(1, LEV_DEV):
        k = kz[lev]
        if lev == LEV_DEV - 1:
            k = jnp.where(place[0] == LEVS - 1, 0.0, k)
        ground = 1.0 + top
        inverse = 1.0 / (series + k + ground)
        below, above = series * inverse, k * inverse
        carry[0, lev - 1] = below
        carry[1, lev - 1] = above
        carry[2, lev - 1] = inverse
        shunt = shunt + below * ground
        top = above * ground
        series = below * k
    ports[0] = shunt
    ports[1] = series
    ports[2] = top


def chunks(array):
    return [array[8 * (w // 2) : 8 * (w // 2) + 8, 128 * (w % 2) : 128 * (w % 2) + 128] for w in range(LEVS)]


def force_body(received, advected, forced):
    data = jnp.concatenate([received[pl.ds(k, TILES, stride=5), :] for k in range(4)], 0)
    where = received[pl.ds(4, TILES, stride=5), :]
    where = jnp.concatenate([where] + [pltpu.roll(where, 128 - 8 * k, 1) for k in range(1, 4)], 0)
    rows_all, lons = data.T, where.T
    lon_id = lax.broadcasted_iota(jnp.int32, (LON, 4 * TILES), 0).astype(F32)
    lat_id = lax.broadcasted_iota(jnp.int32, (4 * TILES, LAT), 1).astype(F32)
    total = jnp.zeros((ROWS * LON, LAT), F32)
    for g in range(8):
        here = lon_id == lons[g : g + 1, :]
        hot = jnp.where(lat_id == where[:, CAP + g : CAP + g + 1], 1.0, 0.0).astype(jnp.bfloat16)
        rows = rows_all[ROWS * g : ROWS * g + ROWS, :]
        coarse = rows.astype(jnp.bfloat16).astype(F32)
        fine = rows - coarse
        for piece in (coarse, fine):
            spread = [jnp.where(here, piece[r : r + 1, :], 0.0).astype(jnp.bfloat16) for r in range(ROWS)]
            total += jnp.dot(jnp.concatenate(spread, 0), hot, preferred_element_type=F32)
    for n in range(ROWS):
        forced[n] = advected[n] + total[n * LON : (n + 1) * LON]


def condense_body(place, forced, first, second, first_own, second_own, carry, ports, inner, blocks):
    even = place[0] % 2 == 0
    row = lax.broadcasted_iota(jnp.int32, (LON, LAT), 0)
    west = jnp.where(even, second[...], first[...])
    east = jnp.where(even, first[...], second[...])
    low_own = jnp.where(even, second_own[...], first_own[...])
    high_own = jnp.where(even, first_own[...], second_own[...])
    for tracer in range(TRACERS):
        full = []
        for lev in range(LEV_DEV):
            n, cx = tracer * LEV_DEV + lev, ROWS + lev
            from_west = -jnp.minimum(west[cx : cx + 1], 0.0) * (west[n : n + 1] - low_own[n : n + 1])
            from_east = jnp.maximum(high_own[cx : cx + 1], 0.0) * (east[n : n + 1] - high_own[n : n + 1])
            across = jnp.where(row == 0, from_west, jnp.where(row == LON - 1, from_east, 0.0))
            full.append(forced[n] + across)
        low = full[0]
        high = jnp.zeros((LON, LAT), F32)
        for lev in range(1, LEV_DEV):
            middle = high + full[lev]
            low = low + carry[0, lev - 1] * middle
            high = carry[1, lev - 1] * middle
            inner[tracer, lev - 1] = carry[2, lev - 1] * middle
        for w, (piece_low, piece_high) in enumerate(zip(chunks(low), chunks(high))):
            blocks[w, tracer] = piece_low
            blocks[w, TRACERS + tracer] = piece_high
    for n in range(3):
        for w, piece in enumerate(chunks(ports[n])):
            blocks[w, 2 * TRACERS + n] = piece


def chain_body(blocks, ends):
    zero = jnp.zeros((8, 128), F32)
    below, rising = [zero], [[zero] * TRACERS]
    for p in range(LEVS - 1):
        shunt, series, top = [blocks[p, 2 * TRACERS + n] for n in range(3)]
        ground = shunt + below[p]
        share = series / (series + ground)
        below.append(top + share * ground)
        rising.append([blocks[p, TRACERS + t] + share * (blocks[p, t] + rising[p][t]) for t in range(TRACERS)])
    above, sinking = zero, [zero] * TRACERS
    for p in range(LEVS - 1, -1, -1):
        shunt, series, top = [blocks[p, 2 * TRACERS + n] for n in range(3)]
        if p == LEVS - 1:
            above, sinking = shunt, [blocks[p, t] for t in range(TRACERS)]
        else:
            ground = top + above
            share = series / (series + ground)
            above = shunt + share * ground
            sinking = [blocks[p, t] + share * (blocks[p, TRACERS + t] + sinking[t]) for t in range(TRACERS)]
        inverse = 1.0 / (below[p] + above)
        for t in range(TRACERS):
            value = (rising[p][t] + sinking[t]) * inverse
            ends[p, t] = value
            if p > 0:
                ends[p - 1, TRACERS + t] = value
            if p == LEVS - 1:
                ends[p, TRACERS + t] = zero


def solve_body(inner, ends, carry, out, result, sems):
    def whole(n):
        return jnp.concatenate([jnp.concatenate([ends[2 * a, n], ends[2 * a + 1, n]], 1) for a in range(4)], 0)

    copies = []
    for tracer in range(TRACERS):
        bottom, level = whole(tracer), whole(TRACERS + tracer)
        for lev in range(LEV_DEV - 1, 0, -1):
            level = inner[tracer, lev - 1] + carry[0, lev - 1] * bottom + carry[1, lev - 1] * level
            result[tracer * LEV_DEV + lev] = level
        result[tracer * LEV_DEV] = bottom
        if tracer % 2 == 1:
            mine = pl.ds((tracer - 1) * LEV_DEV, 2 * LEV_DEV)
            copies.append(pltpu.make_async_copy(result.at[mine], out.at[mine], sems.at[tracer // 2]))
            copies[-1].start()
    for copy in copies:
        copy.wait()


def per_device(adjoint, wind_x, wind_y, kz, forcing, mon_cols, mon_counts):
    place = lax.axis_index("lev").astype(jnp.int32).reshape(1)
    tile = lax.axis_index("tile").astype(jnp.int32).reshape(1)
    field = adjoint.reshape(ROWS, LON, LAT)
    inside = (LEV_DEV - 1, LON, LAT)

    payload, first_own, second_own, advected, carry, ports = pack(
        tile, place, forcing, mon_cols, mon_counts, field, wind_x, wind_y, kz
    )
    second = lax.ppermute(second_own, "tile", [(i, (i + 1 if i % 2 else i - 1) % TILES) for i in range(TILES)])
    first = lax.ppermute(first_own, "tile", [(i, i ^ 1) for i in range(TILES)])
    received = lax.all_to_all(payload.reshape(TILES, 1, 640), "tile", 0, 0, tiled=True).reshape(TILES * 5, 128)
    (forced,) = call(force_body, ((ROWS, LON, LAT),), [VMEM] * 2, limit=24 << 20, moved=2 << 20)(received, advected)
    inner, blocks = call(condense_body, ((TRACERS,) + inside, (LEVS, 11, 8, 128)), [SMEM] + [VMEM] * 7)(
        tile, forced, first, second, first_own, second_own, carry, ports
    )
    arrived = lax.all_to_all(blocks, "lev", 0, 0, tiled=True)
    (ends,) = call(chain_body, ((LEVS, 2 * TRACERS, 8, 128),), [VMEM])(arrived)
    ends = lax.all_to_all(ends, "lev", 0, 0, tiled=True)
    scratch = [pltpu.VMEM((ROWS, LON, LAT), F32), pltpu.SemaphoreType.DMA((TRACERS // 2,))]
    (updated,) = call(solve_body, ((ROWS, LON, LAT),), [VMEM] * 3, scratch, out_spec=HBM)(inner, ends, carry)
    return updated.reshape(adjoint.shape)


def solution(mesh):
    in_specs = (
        P(None, "lev", "tile", None),
        P("lev", "tile", None),
        P("lev", "tile", None),
        P("lev", "tile", None),
        P("tile", None, None, "lev", None),
        P("tile", None, None),
        P("tile", None),
    )
    out_specs = P(None, "lev", "tile", None)
    return jax.shard_map(
        per_device, mesh=mesh, in_specs=in_specs, out_specs=out_specs, check_vma=False
    )
```
